512 devices in a mesh: tok: 64 (over z, y), head: 8 (over x, core).
Axes of the slice: x: 4, y: 4, z: 16, core: 2. Of those that a mesh axis runs over, the one named last changes fastest.
Arguments:
- queries: float32 [16384, 8192], P('tok', 'head'), may hold values from -200 to 200
- keys: float32 [16384, 1024], P('tok', 'head'), may hold values from -6.5 to 6.5
- values: float32 [16384, 1024], P('tok', 'head'), may hold values from -6 to 6
- cotangent: float32 [16384, 8192], P('tok', 'head'), may hold values from -6 to 6
- doc_ids: int32 [16384], P(('tok', 'head')), may hold values from 0 to 127, never falling along the last dimension, each value on 1 to 256 neighbouring positions
Outputs:
- attention_out: float32 [16384, 8192], P('tok', 'head')
- grad_queries: float32 [16384, 8192], P('tok', 'head')
- grad_keys: float32 [16384, 1024], P('tok', 'head')
- grad_values: float32 [16384, 1024], P('tok', 'head')
The draws below stay inside these ranges and needn't reach their ends.
Inputs may be any that keep to these rules, and one draw needn't show every extreme that they name: `doc_ids`: never falling along the sequence; every document has 1 to 256 tokens.
All inputs are finite; a program needn't handle non-finite values.
Results may differ from the reference program's by a relative error of at most 0.0003.
Values sent between devices are 32-bit elements; how exact they have to be, the bound alone decides.
A program may use at most 64 MiB of HBM per device.

```python
import math
import jax
import jax.numpy as jnp
import numpy as np
from jax import lax

HD = 128
GROUP = 8
TOK_DEV = 256
TASKS = 2
KVH = 8
QH = 64
DOC_MOST = 256
WINDOW = 384
TOKENS = 16384
DOCS = 128


def paired_draw(key):
    base = jax.random.fold_in(key, 4242)
    first_key, second_key = jax.random.split(base, 2)
    keys_array = jnp.clip(jax.random.normal(first_key, (TOKENS, KVH, HD), jnp.float32), -6.0, 6.0)
    queries_array = jnp.clip(jax.random.normal(second_key, (TOKENS, KVH, GROUP, HD), jnp.float32), -6.0, 6.0)
    return (queries_array.reshape(TOKENS, KVH * GROUP * HD), keys_array.reshape(TOKENS, KVH * HD))


def draw_queries(key, part):
    return paired_draw(key)[0]


def draw_keys(key, part):
    return paired_draw(key)[1]


def shard_levels(key, shape, pieces, low, high):
    def one(axis_at, shards_of):
        steps = jax.random.uniform(jax.random.fold_in(jax.random.fold_in(key, 6), axis_at), (shards_of,), jnp.float32, low / len(pieces), high / len(pieces))
        return jnp.repeat(jnp.exp(steps), shape[axis_at] // shards_of).reshape((-1,) + (1,) * (len(shape) - axis_at - 1))

    loudness = one(*pieces[0])
    for cut in pieces[1:]:
        loudness = loudness * one(*cut)
    return loudness


def split_up(amount, total, bound, lean):
    weights = [(1 << 20) // math.isqrt(rank ** lean) + 1 for rank in range(2, amount + 1)]
    spare, holding = total - bound - (amount - 1), [1] * (amount - 1)
    while spare > 0:
        candidates = [i for i in range(amount - 1) if holding[i] < bound]
        whole, remaining = sum([weights[i] for i in candidates]), spare
        for i in candidates:
            extra = min(bound - holding[i], max(1, remaining * weights[i] // whole), spare)
            holding[i] = holding[i] + extra
            spare = spare - extra
    return np.array([bound] + holding)


def ragged_sizes(key, amount, total, reach, slope):
    if amount == 2:
        one = jax.random.randint(key, (), max(1, total - reach), min(reach, total - 1) + 1)
        return jnp.stack([one, total - one])
    lengths = jnp.asarray(split_up(amount, total, reach, slope), jnp.int32)
    pairs = (amount - 1) // 2
    source_of, taker = lengths[1:1 + 2 * pairs:2], lengths[2:2 + 2 * pairs:2]
    room = jnp.minimum(source_of - 1, reach - taker)
    moved = jax.random.randint(jax.random.fold_in(key, 1), (pairs,), 0, 1 << 20) % (room + 1)
    lengths = lengths.at[1:1 + 2 * pairs:2].set(source_of - moved).at[2:2 + 2 * pairs:2].set(taker + moved)
    return lengths[jax.random.permutation(jax.random.fold_in(key, 2), amount)]


def bell_draw(key, dims, deviation, limit, shards=(), kind=jnp.bfloat16):
    level = shard_levels(key, dims, shards, -0.22, 0.18) if shards else 1.0
    array = jax.random.normal(key, dims, jnp.float32) * deviation * level
    return jnp.minimum(jnp.maximum(array, -limit), limit).astype(kind)


def setup_inputs(seed: int = 0) -> dict:
    seeds = jax.random.split(jax.random.key(seed), 6)
    return {
        "queries": draw_queries(jax.random.fold_in(seeds[5], 71), 0),
        "keys": draw_keys(jax.random.fold_in(seeds[5], 71), 0),
        "values": bell_draw(seeds[2], (TOKENS, KVH * HD), 1.0, 6.0, ((0, 64), (1, 8)), jnp.float32),
        "cotangent": bell_draw(seeds[3], (TOKENS, QH * HD), 1.0, 6.0, ((0, 64), (1, 8)), jnp.float32),
        "doc_ids": jnp.searchsorted(jnp.cumsum(ragged_sizes(seeds[4], DOCS, TOKENS, DOC_MOST, 2)), jnp.arange(TOKENS), side="right").astype(jnp.int32),
    }


highest = lax.Precision.HIGHEST


def task_attention(query_rows, key_rows, value_rows, grad_rows, query_ids, key_ids):
    score_scale = HD ** -0.5
    query_pos = jnp.arange(query_rows.shape[0], dtype=jnp.int32)[:, None]
    key_pos = jnp.arange(key_rows.shape[0], dtype=jnp.int32)[None, :]
    allowed = (key_ids[None, :] == query_ids[:, None]) & (key_ids[None, :] > 0) & (key_pos <= query_pos + DOC_MOST)
    scores = jnp.einsum("qcgd,kcd->cgqk", query_rows, key_rows, precision=highest) * score_scale
    scores = jnp.where(allowed, scores, -1e30)
    top_score = jnp.max(scores, axis=-1, keepdims=True)
    weights = jnp.where(allowed, jnp.exp(scores - top_score), 0.0)
    probs = weights / jnp.sum(weights, axis=-1, keepdims=True)
    output = jnp.einsum("cgqk,kcd->qcgd", probs, value_rows, precision=highest)
    row_delta = jnp.transpose(jnp.sum(grad_rows * output, axis=-1), (1, 2, 0))
    grad_values = jnp.einsum("cgqk,qcgd->kcd", probs, grad_rows, precision=highest)
    grad_probs = jnp.einsum("qcgd,kcd->cgqk", grad_rows, value_rows, precision=highest)
    grad_scores = probs * (grad_probs - row_delta[..., None])
    grad_queries = score_scale * jnp.einsum("cgqk,kcd->qcgd", grad_scores, key_rows, precision=highest)
    grad_keys = score_scale * jnp.einsum("cgqk,qcgd->kcd", grad_scores, query_rows, precision=highest)
    return output, grad_queries, grad_keys, grad_values


def reference(queries, keys, values, cotangent, doc_ids):
    task_rows = TOK_DEV // TASKS
    task_total = TOKENS // task_rows
    shaped_queries = queries.reshape(TOKENS, KVH, GROUP, HD)
    shaped_grads = cotangent.reshape(TOKENS, KVH, GROUP, HD)
    padding = jnp.zeros((DOC_MOST, KVH, HD), keys.dtype)
    padded_keys = jnp.concatenate([padding, keys.reshape(TOKENS, KVH, HD)], axis=0)
    padded_values = jnp.concatenate([padding, values.reshape(TOKENS, KVH, HD)], axis=0)
    padded_ids = jnp.concatenate([jnp.zeros((DOC_MOST,), jnp.int32), doc_ids.astype(jnp.int32) + 1], axis=0)

    def one_task(carried, task_index):
        key_grad, value_grad = carried
        row_start = (task_index * task_rows).astype(jnp.int32)
        query_rows = lax.dynamic_slice_in_dim(shaped_queries, row_start, task_rows, 0)
        grad_rows = lax.dynamic_slice_in_dim(shaped_grads, row_start, task_rows, 0)
        key_rows = lax.dynamic_slice_in_dim(padded_keys, row_start, WINDOW, 0)
        value_rows = lax.dynamic_slice_in_dim(padded_values, row_start, WINDOW, 0)
        key_ids = lax.dynamic_slice_in_dim(padded_ids, row_start, WINDOW, 0)
        query_ids = lax.dynamic_slice_in_dim(padded_ids, (row_start + DOC_MOST).astype(jnp.int32), task_rows, 0)
        output, grad_queries, grad_keys, grad_values = task_attention(query_rows, key_rows, value_rows, grad_rows, query_ids, key_ids)
        key_grad = lax.dynamic_update_slice_in_dim(key_grad, lax.dynamic_slice_in_dim(key_grad, row_start, WINDOW, 0) + grad_keys, row_start, 0)
        value_grad = lax.dynamic_update_slice_in_dim(value_grad, lax.dynamic_slice_in_dim(value_grad, row_start, WINDOW, 0) + grad_values, row_start, 0)
        return (key_grad, value_grad), (output, grad_queries)

    start_grads = (jnp.zeros_like(padded_keys), jnp.zeros_like(padded_values))
    (key_grad, value_grad), (outputs, query_grads) = lax.scan(one_task, start_grads, jnp.arange(task_total, dtype=jnp.int32))
    attention_out = outputs.reshape(TOKENS, QH * HD)
    grad_queries = query_grads.reshape(TOKENS, QH * HD)
    grad_keys = key_grad[DOC_MOST:].reshape(TOKENS, KVH * HD)
    grad_values = value_grad[DOC_MOST:].reshape(TOKENS, KVH * HD)
    return attention_out, grad_queries, grad_keys, grad_values
```

```python
import functools
import math

import jax
import jax.numpy as jnp
from jax import lax
from jax.experimental import pallas as pl
from jax.experimental.pallas import tpu as pltpu
from jax.sharding import PartitionSpec as P

HEAD_DIM = 128
TILE = 128
PAIRS = 4
TASKS = 2
IDS = 32
MESH = pl.DeviceIdType.MESH
SCORE_SCALE = HEAD_DIM**-0.5
LOG2E = math.log2(math.e)
NEG = -1e30

f32 = jnp.float32
bf16 = jnp.bfloat16


def parts2(x):
    high = x.astype(bf16)
    low = (x - high.astype(f32)).astype(bf16)
    return high, low


def parts3(x):
    high = x.astype(bf16)
    rest = x - high.astype(f32)
    mid = rest.astype(bf16)
    low = (rest - mid.astype(f32)).astype(bf16)
    return high, mid, low


def lanes(*xs):
    return jnp.concatenate(xs, axis=1)


def rows(*xs):
    return jnp.concatenate(xs, axis=0)


def dot_nn(a, b):
    return lax.dot_general(a, b, (((1,), (0,)), ((), ())), preferred_element_type=f32)


def dot_nt(a, b):
    return lax.dot_general(a, b, (((1,), (1,)), ((), ())), preferred_element_type=f32)


def kernel(
    tok_count,
    head_count,
    q_hbm,
    k_hbm,
    v_hbm,
    g_hbm,
    ids_ref,
    o_ref,
    dq_ref,
    dk_ref,
    dv_ref,
    qf,
    gf,
    k_own,
    v_own,
    k_prev,
    v_prev,
    gk_out,
    gv_out,
    gk_in,
    gv_in,
    id_mine,
    id_got,
    id_own,
    id_prev,
    bias,
    qp,
    gp,
    kc,
    vc,
    kt,
    vt,
    s_own,
    dp_own,
    pf,
    p1,
    p2,
    ds1,
    ds2,
    acc_k,
    acc_v,
    local_sem,
    send_sem,
    recv_sem,
    id_send_sem,
    id_recv_sem,
):
    tok = lax.axis_index("tok")
    head = lax.axis_index("head")
    nxt = (lax.rem(tok + 1, tok_count), head)
    prv = (lax.rem(tok + tok_count - 1, tok_count), head)
    peers = [(tok, lax.rem(head + j, head_count)) for j in range(1, head_count)]

    loads = [
        pltpu.make_async_copy(src, dst, local_sem.at[i])
        for i, (src, dst) in enumerate(
            [(k_hbm, k_own), (v_hbm, v_own), (q_hbm, qf), (g_hbm, gf)]
        )
    ]
    for load in loads:
        load.start()

    barrier = pltpu.get_barrier_semaphore()
    for device in [nxt, prv, *peers]:
        pl.semaphore_signal(barrier, inc=1, device_id=device, device_id_type=MESH)

    spread = (
        lax.broadcasted_iota(jnp.int32, (IDS, TILE), 1) % IDS
        == lax.broadcasted_iota(jnp.int32, (IDS, TILE), 0)
    )
    ids = jnp.broadcast_to(ids_ref[...].astype(f32), (8, IDS)).astype(bf16)
    id_mine[...] = dot_nn(ids, jnp.where(spread, 1.0, 0.0).astype(bf16))
    id_got[head] = id_mine[...]

    pl.semaphore_wait(barrier, head_count + 1)

    id_copies = [
        pltpu.make_async_remote_copy(
            src_ref=id_mine,
            dst_ref=id_got.at[head],
            send_sem=id_send_sem.at[j],
            recv_sem=id_recv_sem.at[j],
            device_id=device,
            device_id_type=MESH,
        )
        for j, device in enumerate(peers)
    ]
    for copy in id_copies:
        copy.start()

    def to(device, i, src, dst):
        return pltpu.make_async_remote_copy(
            src_ref=src,
            dst_ref=dst,
            send_sem=send_sem.at[i],
            recv_sem=recv_sem.at[i],
            device_id=device,
            device_id_type=MESH,
        )

    send_k = to(nxt, 0, k_hbm, k_prev)
    send_v = to(nxt, 1, v_hbm, v_prev)
    send_id = to(nxt, 2, id_own, id_prev)
    send_gk = to(prv, 3, gk_out, gk_in)
    send_gv = to(prv, 4, gv_out, gv_in)
    send_k.start()

    def pack_k(k, base):
        a, b, c = parts3(k)
        kc[base : base + 2 * TILE] = lanes(a, a, b, b, c, a)
        kt[:, base : base + 2 * TILE] = rows(*parts2(k.T))

    def pack_v(v, base):
        a, b = parts2(v)
        vc[base : base + 2 * TILE] = lanes(a, a, b, b)
        vt[:, base : base + 2 * TILE] = rows(*parts2(v.T))

    loads[0].wait()
    loads[1].wait()
    pack_k(k_own[...], 2 * TILE)
    pack_v(v_own[...], 2 * TILE)
    loads[2].wait()
    loads[3].wait()

    def q_pack(t, pair):
        a, b, c = (qp[t, pair, :, i * TILE : (i + 1) * TILE] for i in range(3))
        return lanes(a, b, a, b, a, c)

    def g_pack(t, pair):
        g = gp[t, pair]
        return lanes(g, g)

    def own_scores(pair, _):
        columns = pl.ds(pl.multiple_of(pair * 2 * TILE, 2 * TILE), 2 * TILE)
        for t in range(TASKS):
            of_task = slice(t * TILE, (t + 1) * TILE)
            q = qf[of_task, columns] * (SCORE_SCALE * LOG2E)
            qp[t, pair] = lanes(*parts3(rows(q[:, :TILE], q[:, TILE:])))
            g = gf[of_task, columns]
            gp[t, pair] = lanes(*parts2(rows(g[:, :TILE], g[:, TILE:])))
            own = slice(2 * TILE, (3 + t) * TILE)
            kept = slice(t * TILE, (1 + 2 * t) * TILE)
            s_own[pair, kept] = dot_nt(kc[own], q_pack(t, pair))
            dp_own[pair, kept] = dot_nt(vc[own], g_pack(t, pair))
        return 0

    lax.fori_loop(0, PAIRS, own_scores, 0)

    for copy in id_copies:
        copy.wait_recv()
    lane_group = lax.broadcasted_iota(jnp.int32, (8, TILE), 1) // IDS
    for t in range(TASKS):
        row = id_got[4 * t]
        for j in range(1, TILE // IDS):
            row = jnp.where(lane_group == j, id_got[4 * t + j], row)
        id_own[t] = row
    send_id.start()
    send_v.start()

    send_id.wait_recv()
    id_rows = [jnp.where(tok == 0, -1.0, id_prev[t]) for t in range(TASKS)]
    id_rows += [id_own[t] for t in range(TASKS)]
    wide = [jnp.broadcast_to(r[0:1], (TILE, TILE)) for r in id_rows]
    causal = lax.broadcasted_iota(jnp.int32, (TILE, TILE), 0) <= lax.broadcasted_iota(
        jnp.int32, (TILE, TILE), 1
    )
    for t in range(TASKS):
        for j in range(3):
            allowed = wide[t + j].T == wide[2 + t]
            if j == 2:
                allowed = allowed & causal
            bias[t, j * TILE : (j + 1) * TILE] = jnp.where(allowed, 0.0, NEG)

    send_k.wait_recv()
    pack_k(k_prev[...], 0)

    acc_k[...] = jnp.zeros_like(acc_k)
    acc_v[...] = jnp.zeros_like(acc_v)

    def probs(pair, _):
        for t in range(TASKS):
            before = slice(t * TILE, 2 * TILE)
            kept = slice(t * TILE, (1 + 2 * t) * TILE)
            b = bias[t]
            s = rows(dot_nt(kc[before], q_pack(t, pair)), s_own[pair, kept]) + lanes(b, b)
            weights = jnp.exp2(s - jnp.max(s, axis=0, keepdims=True))
            p = weights * (1.0 / jnp.sum(weights, axis=0, keepdims=True))
            pf[t, pair] = p
            high, low = parts2(p)
            p1[t, pair] = high
            p2[t, pair] = low
            g = gp[t, pair]
            ahead = (2 - t) * TILE
            acc_v[before] += dot_nn(lanes(high[:ahead], low[:ahead]), rows(g, g))
        return 0

    lax.fori_loop(0, PAIRS, probs, 0)
    gv_out[...] = acc_v[: 2 * TILE, :TILE] + acc_v[: 2 * TILE, TILE:]
    send_gv.start()

    def own_values(pair, _):
        for t in range(TASKS):
            own = slice(2 * TILE, (3 + t) * TILE)
            ahead = (2 - t) * TILE
            g = gp[t, pair]
            acc_v[own] += dot_nn(lanes(p1[t, pair, ahead:], p2[t, pair, ahead:]), rows(g, g))
        return 0

    lax.fori_loop(0, PAIRS, own_values, 0)

    send_v.wait_recv()
    pack_v(v_prev[...], 0)

    def grads(pair, _):
        for t in range(TASKS):
            before = slice(t * TILE, 2 * TILE)
            kept = slice(t * TILE, (1 + 2 * t) * TILE)
            dp = rows(dot_nt(vc[before], g_pack(t, pair)), dp_own[pair, kept])
            p = pf[t, pair]
            delta = jnp.sum(p * dp, axis=0, keepdims=True)
            high, low = parts2(p * (dp - delta))
            ds1[t, pair] = high
            ds2[t, pair] = low
            q = qp[t, pair, :, : 2 * TILE]
            ahead = (2 - t) * TILE
            acc_k[before] += dot_nn(lanes(high[:ahead], low[:ahead]), rows(q, q))
        return 0

    lax.fori_loop(0, PAIRS, grads, 0)
    gk_out[...] = (acc_k[: 2 * TILE, :TILE] + acc_k[: 2 * TILE, TILE:]) * (1.0 / LOG2E)
    send_gk.start()

    def results(pair, _):
        for t in range(TASKS):
            own = slice(2 * TILE, (3 + t) * TILE)
            ahead = (2 - t) * TILE
            q = qp[t, pair, :, : 2 * TILE]
            acc_k[own] += dot_nn(lanes(ds1[t, pair, ahead:], ds2[t, pair, ahead:]), rows(q, q))
            window = slice(t * TILE, (t + 3) * TILE)
            of_task = slice(t * TILE, (t + 1) * TILE)
            for mat, high, low, out, scale in (
                (vt, p1, p2, o_ref, None),
                (kt, ds1, ds2, dq_ref, SCORE_SCALE),
            ):
                m = mat[:, window]
                both = dot_nn(lanes(m, m), rows(high[t, pair], low[t, pair]))
                x = both[:TILE] + both[TILE:]
                if scale is not None:
                    x = x * scale
                for h in range(2):
                    columns = pl.ds(
                        pl.multiple_of(pair * 2 * TILE + h * TILE, TILE), TILE
                    )
                    out[of_task, columns] = x[:, h * TILE : (h + 1) * TILE].T
        return 0

    lax.fori_loop(0, PAIRS, results, 0)

    send_gv.wait_recv()
    dv_ref[...] = acc_v[2 * TILE :, :TILE] + acc_v[2 * TILE :, TILE:] + gv_in[...]
    send_gk.wait_recv()
    dk_ref[...] = (acc_k[2 * TILE :, :TILE] + acc_k[2 * TILE :, TILE:]) * (
        1.0 / LOG2E
    ) + gk_in[...]
    for copy in [*id_copies, send_k, send_v, send_id, send_gk, send_gv]:
        copy.wait_send()


def per_device(queries, keys, values, cotangent, doc_ids):
    tok_count = lax.axis_size("tok")
    head_count = lax.axis_size("head")
    vmem = pl.BlockSpec(memory_space=pltpu.VMEM)
    hbm = pl.BlockSpec(memory_space=pl.ANY)
    own = 2 * TILE
    win = 3 * TILE
    V = pltpu.VMEM
    return pl.pallas_call(
        functools.partial(kernel, tok_count, head_count),
        out_shape=(
            jax.ShapeDtypeStruct(queries.shape, f32),
            jax.ShapeDtypeStruct(queries.shape, f32),
            jax.ShapeDtypeStruct(keys.shape, f32),
            jax.ShapeDtypeStruct(keys.shape, f32),
        ),
        in_specs=[hbm, hbm, hbm, hbm, vmem],
        out_specs=(vmem, vmem, vmem, vmem),
        scratch_shapes=[
            V(queries.shape, f32),
            V(queries.shape, f32),
            *[V(keys.shape, f32) for _ in range(8)],
            V((8, TILE), f32),
            V((head_count, 8, TILE), f32),
            V((TASKS, 8, TILE), f32),
            V((TASKS, 8, TILE), f32),
            V((TASKS, win, TILE), f32),
            V((TASKS, PAIRS, own, 3 * TILE), bf16),
            V((TASKS, PAIRS, own, 2 * TILE), bf16),
            V((2 * own, 6 * TILE), bf16),
            V((2 * own, 4 * TILE), bf16),
            V((2 * TILE, 2 * own), bf16),
            V((2 * TILE, 2 * own), bf16),
            V((PAIRS, win, own), f32),
            V((PAIRS, win, own), f32),
            V((TASKS, PAIRS, win, own), f32),
            *[V((TASKS, PAIRS, win, own), bf16) for _ in range(4)],
            V((2 * own, 2 * TILE), f32),
            V((2 * own, 2 * TILE), f32),
            pltpu.SemaphoreType.DMA((4,)),
            pltpu.SemaphoreType.DMA((5,)),
            pltpu.SemaphoreType.DMA((5,)),
            pltpu.SemaphoreType.DMA((head_count - 1,)),
            pltpu.SemaphoreType.DMA((head_count - 1,)),
        ],
        compiler_params=pltpu.CompilerParams(
            collective_id=0, has_side_effects=True, vmem_limit_bytes=40 * 1024 * 1024
        ),
    )(queries, keys, values, cotangent, doc_ids.reshape(1, IDS))


def solution(mesh):
    placed = (
        P("tok", "head"),
        P("tok", "head"),
        P("tok", "head"),
        P("tok", "head"),
        P(("tok", "head")),
    )
    return jax.shard_map(
        per_device,
        mesh=mesh,
        in_specs=placed,
        out_specs=(P("tok", "head"), P("tok", "head"), P("tok", "head"), P("tok", "head")),
        check_vma=False,
    )
```

```python
import functools
import math

import jax
import jax.numpy as jnp
from jax import lax
from jax.experimental import pallas as pl
from jax.experimental.pallas import tpu as pltpu
from jax.sharding import PartitionSpec as P

HEAD_DIM = 128
TILE = 128
PAIRS = 4
TASKS = 2
IDS = 32
MESH = pl.DeviceIdType.MESH
SCORE_SCALE = HEAD_DIM**-0.5
LOG2E = math.log2(math.e)
NEG = -1e30

f32 = jnp.float32
bf16 = jnp.bfloat16


def parts2(x):
    high = x.astype(bf16)
    low = (x - high.astype(f32)).astype(bf16)
    return high, low


def parts3(x):
    high = x.astype(bf16)
    rest = x - high.astype(f32)
    mid = rest.astype(bf16)
    low = (rest - mid.astype(f32)).astype(bf16)
    return high, mid, low


def lanes(*xs):
    return jnp.concatenate(xs, axis=1)


def rows(*xs):
    return jnp.concatenate(xs, axis=0)


def dot_nn(a, b):
    return lax.dot_general(a, b, (((1,), (0,)), ((), ())), preferred_element_type=f32)


def dot_nt(a, b):
    return lax.dot_general(a, b, (((1,), (1,)), ((), ())), preferred_element_type=f32)


def kernel(
    tok_count,
    head_count,
    q_hbm,
    k_hbm,
    v_hbm,
    g_hbm,
    ids_hbm,
    o_ref,
    dq_ref,
    dk_ref,
    dv_ref,
    qf,
    gf,
    k_own,
    v_own,
    k_prev,
    v_prev,
    gk_out,
    gv_out,
    gk_in,
    gv_in,
    id_raw,
    id_mine,
    id_got,
    id_own,
    id_prev,
    bias,
    qp,
    gp,
    kc,
    vc,
    kt,
    vt,
    s_own,
    dp_own,
    pf,
    p1,
    p2,
    ds1,
    ds2,
    acc_k,
    acc_v,
    local_sem,
    send_sem,
    recv_sem,
    id_send_sem,
    id_recv_sem,
):
    tok = lax.axis_index("tok")
    head = lax.axis_index("head")
    nxt = (lax.rem(tok + 1, tok_count), head)
    prv = (lax.rem(tok + tok_count - 1, tok_count), head)
    peers = [(tok, lax.rem(head + j, head_count)) for j in range(1, head_count)]

    loads = [
        pltpu.make_async_copy(src, dst, local_sem.at[i])
        for i, (src, dst) in enumerate(
            [(ids_hbm, id_raw), (k_hbm, k_own), (v_hbm, v_own), (q_hbm, qf), (g_hbm, gf)]
        )
    ]
    for load in loads:
        load.start()

    barrier = pltpu.get_barrier_semaphore()
    for device in [nxt, prv, *peers]:
        pl.semaphore_signal(barrier, inc=1, device_id=device, device_id_type=MESH)

    spread = (
        lax.broadcasted_iota(jnp.int32, (IDS, TILE), 1) % IDS
        == lax.broadcasted_iota(jnp.int32, (IDS, TILE), 0)
    )
    loads[0].wait()
    ids = jnp.broadcast_to(id_raw[...].astype(f32), (8, IDS)).astype(bf16)
    id_mine[...] = dot_nn(ids, jnp.where(spread, 1.0, 0.0).astype(bf16))
    id_got[head] = id_mine[...]

    pl.semaphore_wait(barrier, head_count + 1)

    id_copies = [
        pltpu.make_async_remote_copy(
            src_ref=id_mine,
            dst_ref=id_got.at[head],
            send_sem=id_send_sem.at[j],
            recv_sem=id_recv_sem.at[j],
            device_id=device,
            device_id_type=MESH,
        )
        for j, device in enumerate(peers)
    ]
    for copy in id_copies:
        copy.start()

    def to(device, i, src, dst):
        return pltpu.make_async_remote_copy(
            src_ref=src,
            dst_ref=dst,
            send_sem=send_sem.at[i],
            recv_sem=recv_sem.at[i],
            device_id=device,
            device_id_type=MESH,
        )

    send_k = to(nxt, 0, k_hbm, k_prev)
    send_v = to(nxt, 1, v_hbm, v_prev)
    send_id = to(nxt, 2, id_own, id_prev)
    send_gk = to(prv, 3, gk_out, gk_in)
    send_gv = to(prv, 4, gv_out, gv_in)
    send_k.start()

    def pack_k(k, base):
        a, b, c = parts3(k)
        kc[base : base + 2 * TILE] = lanes(a, a, b, b, c, a)
        kt[:, base : base + 2 * TILE] = rows(*parts2(k.T))

    def pack_v(v, base):
        a, b = parts2(v)
        vc[base : base + 2 * TILE] = lanes(a, a, b, b)
        vt[:, base : base + 2 * TILE] = rows(*parts2(v.T))

    loads[1].wait()
    loads[2].wait()
    pack_k(k_own[...], 2 * TILE)
    pack_v(v_own[...], 2 * TILE)
    loads[3].wait()
    loads[4].wait()

    def q_pack(t, pair):
        a, b, c = (qp[t, pair, :, i * TILE : (i + 1) * TILE] for i in range(3))
        return lanes(a, b, a, b, a, c)

    def g_pack(t, pair):
        g = gp[t, pair]
        return lanes(g, g)

    def own_scores(pair, _):
        columns = pl.ds(pl.multiple_of(pair * 2 * TILE, 2 * TILE), 2 * TILE)
        for t in range(TASKS):
            of_task = slice(t * TILE, (t + 1) * TILE)
            q = qf[of_task, columns] * (SCORE_SCALE * LOG2E)
            qp[t, pair] = lanes(*parts3(rows(q[:, :TILE], q[:, TILE:])))
            g = gf[of_task, columns]
            gp[t, pair] = lanes(*parts2(rows(g[:, :TILE], g[:, TILE:])))
            own = slice(2 * TILE, (3 + t) * TILE)
            kept = slice(t * TILE, (1 + 2 * t) * TILE)
            s_own[pair, kept] = dot_nt(kc[own], q_pack(t, pair))
            dp_own[pair, kept] = dot_nt(vc[own], g_pack(t, pair))
        return 0

    lax.fori_loop(0, PAIRS, own_scores, 0, unroll=True)

    for copy in id_copies:
        copy.wait_recv()
    lane_group = lax.broadcasted_iota(jnp.int32, (8, TILE), 1) // IDS
    for t in range(TASKS):
        row = id_got[4 * t]
        for j in range(1, TILE // IDS):
            row = jnp.where(lane_group == j, id_got[4 * t + j], row)
        id_own[t] = row
    send_id.start()
    send_v.start()

    send_id.wait_recv()
    id_rows = [jnp.where(tok == 0, -1.0, id_prev[t]) for t in range(TASKS)]
    id_rows += [id_own[t] for t in range(TASKS)]
    wide = [jnp.broadcast_to(r[0:1], (TILE, TILE)) for r in id_rows]
    causal = lax.broadcasted_iota(jnp.int32, (TILE, TILE), 0) <= lax.broadcasted_iota(
        jnp.int32, (TILE, TILE), 1
    )
    for t in range(TASKS):
        for j in range(3):
            allowed = wide[t + j].T == wide[2 + t]
            if j == 2:
                allowed = allowed & causal
            bias[t, j * TILE : (j + 1) * TILE] = jnp.where(allowed, 0.0, NEG)

    send_k.wait_recv()
    pack_k(k_prev[...], 0)

    acc_k[...] = jnp.zeros_like(acc_k)
    acc_v[...] = jnp.zeros_like(acc_v)

    def probs(pair, _):
        for t in range(TASKS):
            before = slice(t * TILE, 2 * TILE)
            kept = slice(t * TILE, (1 + 2 * t) * TILE)
            b = bias[t]
            s = rows(dot_nt(kc[before], q_pack(t, pair)), s_own[pair, kept]) + lanes(b, b)
            weights = jnp.exp2(s - jnp.max(s, axis=0, keepdims=True))
            p = weights * (1.0 / jnp.sum(weights, axis=0, keepdims=True))
            pf[t, pair] = p
            high, low = parts2(p)
            p1[t, pair] = high
            p2[t, pair] = low
            g = gp[t, pair]
            ahead = (2 - t) * TILE
            acc_v[before] += dot_nn(lanes(high[:ahead], low[:ahead]), rows(g, g))
        return 0

    lax.fori_loop(0, PAIRS, probs, 0, unroll=True)
    gv_out[...] = acc_v[: 2 * TILE, :TILE] + acc_v[: 2 * TILE, TILE:]
    send_gv.start()

    def own_values(pair, _):
        for t in range(TASKS):
            own = slice(2 * TILE, (3 + t) * TILE)
            ahead = (2 - t) * TILE
            g = gp[t, pair]
            acc_v[own] += dot_nn(lanes(p1[t, pair, ahead:], p2[t, pair, ahead:]), rows(g, g))
        return 0

    lax.fori_loop(0, PAIRS, own_values, 0, unroll=True)

    send_v.wait_recv()
    pack_v(v_prev[...], 0)

    def grads(pair, _):
        for t in range(TASKS):
            before = slice(t * TILE, 2 * TILE)
            kept = slice(t * TILE, (1 + 2 * t) * TILE)
            dp = rows(dot_nt(vc[before], g_pack(t, pair)), dp_own[pair, kept])
            p = pf[t, pair]
            delta = jnp.sum(p * dp, axis=0, keepdims=True)
            high, low = parts2(p * (dp - delta))
            ds1[t, pair] = high
            ds2[t, pair] = low
            q = qp[t, pair, :, : 2 * TILE]
            ahead = (2 - t) * TILE
            acc_k[before] += dot_nn(lanes(high[:ahead], low[:ahead]), rows(q, q))
        return 0

    lax.fori_loop(0, PAIRS, grads, 0, unroll=True)
    gk_out[...] = (acc_k[: 2 * TILE, :TILE] + acc_k[: 2 * TILE, TILE:]) * (1.0 / LOG2E)
    send_gk.start()

    def results(pair, _):
        for t in range(TASKS):
            own = slice(2 * TILE, (3 + t) * TILE)
            ahead = (2 - t) * TILE
            q = qp[t, pair, :, : 2 * TILE]
            acc_k[own] += dot_nn(lanes(ds1[t, pair, ahead:], ds2[t, pair, ahead:]), rows(q, q))
            window = slice(t * TILE, (t + 3) * TILE)
            of_task = slice(t * TILE, (t + 1) * TILE)
            for mat, high, low, out, scale in (
                (vt, p1, p2, o_ref, None),
                (kt, ds1, ds2, dq_ref, SCORE_SCALE),
            ):
                m = mat[:, window]
                both = dot_nn(lanes(m, m), rows(high[t, pair], low[t, pair]))
                x = both[:TILE] + both[TILE:]
                if scale is not None:
                    x = x * scale
                for h in range(2):
                    columns = pl.ds(
                        pl.multiple_of(pair * 2 * TILE + h * TILE, TILE), TILE
                    )
                    out[of_task, columns] = x[:, h * TILE : (h + 1) * TILE].T
        return 0

    lax.fori_loop(0, PAIRS, results, 0, unroll=True)

    send_gv.wait_recv()
    dv_ref[...] = acc_v[2 * TILE :, :TILE] + acc_v[2 * TILE :, TILE:] + gv_in[...]
    send_gk.wait_recv()
    dk_ref[...] = (acc_k[2 * TILE :, :TILE] + acc_k[2 * TILE :, TILE:]) * (
        1.0 / LOG2E
    ) + gk_in[...]
    for copy in [*id_copies, send_k, send_v, send_id, send_gk, send_gv]:
        copy.wait_send()


def place(a, b, c, d, a_out, b_out, c_out, d_out, sem):
    copies = [
        pltpu.make_async_copy(src, dst, sem.at[i])
        for i, (src, dst) in enumerate([(a, a_out), (b, b_out), (c, c_out), (d, d_out)])
    ]
    for copy in copies:
        copy.start()
    for copy in copies:
        copy.wait()


def per_device(queries, keys, values, cotangent, doc_ids):
    tok_count = lax.axis_size("tok")
    head_count = lax.axis_size("head")
    vmem = pl.BlockSpec(memory_space=pltpu.VMEM)
    hbm = pl.BlockSpec(memory_space=pl.ANY)
    own = 2 * TILE
    win = 3 * TILE
    V = pltpu.VMEM
    found = pl.pallas_call(
        functools.partial(kernel, tok_count, head_count),
        out_shape=(
            jax.ShapeDtypeStruct(queries.shape, f32),
            jax.ShapeDtypeStruct(queries.shape, f32),
            jax.ShapeDtypeStruct(keys.shape, f32),
            jax.ShapeDtypeStruct(keys.shape, f32),
        ),
        in_specs=[hbm] * 5,
        out_specs=(vmem, vmem, vmem, vmem),
        scratch_shapes=[
            V(queries.shape, f32),
            V(queries.shape, f32),
            *[V(keys.shape, f32) for _ in range(8)],
            V((1, IDS), jnp.int32),
            V((8, TILE), f32),
            V((head_count, 8, TILE), f32),
            V((TASKS, 8, TILE), f32),
            V((TASKS, 8, TILE), f32),
            V((TASKS, win, TILE), f32),
            V((TASKS, PAIRS, own, 3 * TILE), bf16),
            V((TASKS, PAIRS, own, 2 * TILE), bf16),
            V((2 * own, 6 * TILE), bf16),
            V((2 * own, 4 * TILE), bf16),
            V((2 * TILE, 2 * own), bf16),
            V((2 * TILE, 2 * own), bf16),
            V((PAIRS, win, own), f32),
            V((PAIRS, win, own), f32),
            V((TASKS, PAIRS, win, own), f32),
            *[V((TASKS, PAIRS, win, own), bf16) for _ in range(4)],
            V((2 * own, 2 * TILE), f32),
            V((2 * own, 2 * TILE), f32),
            pltpu.SemaphoreType.DMA((5,)),
            pltpu.SemaphoreType.DMA((5,)),
            pltpu.SemaphoreType.DMA((5,)),
            pltpu.SemaphoreType.DMA((head_count - 1,)),
            pltpu.SemaphoreType.DMA((head_count - 1,)),
        ],
        compiler_params=pltpu.CompilerParams(
            collective_id=0, has_side_effects=True, vmem_limit_bytes=40 * 1024 * 1024
        ),
    )(
        *(
            pltpu.with_memory_space_constraint(x, pltpu.HBM)
            for x in (queries, keys, values, cotangent, doc_ids.reshape(1, IDS))
        )
    )
    return pl.pallas_call(
        place,
        out_shape=tuple(jax.ShapeDtypeStruct(x.shape, f32) for x in found),
        in_specs=[hbm] * 4,
        out_specs=(hbm,) * 4,
        scratch_shapes=[pltpu.SemaphoreType.DMA((4,))],
        compiler_params=pltpu.CompilerParams(vmem_limit_bytes=1024 * 1024),
    )(*found)


def solution(mesh):
    placed = (
        P("tok", "head"),
        P("tok", "head"),
        P("tok", "head"),
        P("tok", "head"),
        P(("tok", "head")),
    )
    return jax.shard_map(
        per_device,
        mesh=mesh,
        in_specs=placed,
        out_specs=(P("tok", "head"), P("tok", "head"), P("tok", "head"), P("tok", "head")),
        check_vma=False,
    )
```

```python
import functools
import math

import jax
import jax.numpy as jnp
from jax import lax
from jax.experimental import pallas as pl
from jax.experimental.pallas import tpu as pltpu
from jax.sharding import PartitionSpec as P

HEAD_DIM = 128
TILE = 128
PAIRS = 4
TASKS = 2
IDS = 32
MESH = pl.DeviceIdType.MESH
SCORE_SCALE = HEAD_DIM**-0.5
LOG2E = math.log2(math.e)
NEG = -1e30

f32 = jnp.float32
bf16 = jnp.bfloat16


def parts2(x):
    high = x.astype(bf16)
    low = (x - high.astype(f32)).astype(bf16)
    return high, low


def parts3(x):
    high = x.astype(bf16)
    rest = x - high.astype(f32)
    mid = rest.astype(bf16)
    low = (rest - mid.astype(f32)).astype(bf16)
    return high, mid, low


def lanes(*xs):
    return jnp.concatenate(xs, axis=1)


def rows(*xs):
    return jnp.concatenate(xs, axis=0)


def dot_nn(a, b):
    return lax.dot_general(a, b, (((1,), (0,)), ((), ())), preferred_element_type=f32)


def dot_nt(a, b):
    return lax.dot_general(a, b, (((1,), (1,)), ((), ())), preferred_element_type=f32)


def kernel(
    tok_count,
    head_count,
    q_hbm,
    k_hbm,
    v_hbm,
    g_hbm,
    ids_hbm,
    o_ref,
    dq_ref,
    dk_ref,
    dv_ref,
    qf,
    gf,
    k_own,
    v_own,
    k_prev,
    v_prev,
    gk_out,
    gv_out,
    gk_in,
    gv_in,
    id_raw,
    id_mine,
    id_got,
    id_own,
    id_prev,
    bias,
    qp,
    gp,
    kc,
    vc,
    kt,
    vt,
    s_own,
    dp_own,
    pf,
    p1,
    p2,
    ds1,
    ds2,
    acc_k,
    acc_v,
    local_sem,
    send_sem,
    recv_sem,
    id_send_sem,
    id_recv_sem,
):
    tok = lax.axis_index("tok")
    head = lax.axis_index("head")
    nxt = (lax.rem(tok + 1, tok_count), head)
    prv = (lax.rem(tok + tok_count - 1, tok_count), head)
    peers = [(tok, lax.rem(head + j, head_count)) for j in range(1, head_count)]

    loads = [
        pltpu.make_async_copy(src, dst, local_sem.at[i])
        for i, (src, dst) in enumerate(
            [(ids_hbm, id_raw), (k_hbm, k_own), (v_hbm, v_own), (q_hbm, qf), (g_hbm, gf)]
        )
    ]
    for load in loads:
        load.start()

    has_prev = tok > 0
    has_next = tok < tok_count - 1

    barrier = pltpu.get_barrier_semaphore()

    def greet(device):
        pl.semaphore_signal(barrier, inc=1, device_id=device, device_id_type=MESH)

    pl.when(has_next)(lambda: greet(nxt))
    pl.when(has_prev)(lambda: greet(prv))
    for device in peers:
        greet(device)

    @pl.when(jnp.logical_not(has_prev))
    def _():
        k_prev[...] = jnp.zeros_like(k_prev)
        v_prev[...] = jnp.zeros_like(v_prev)
        id_prev[...] = jnp.full_like(id_prev, -1.0)

    @pl.when(jnp.logical_not(has_next))
    def _():
        gk_in[...] = jnp.zeros_like(gk_in)
        gv_in[...] = jnp.zeros_like(gv_in)

    spread = (
        lax.broadcasted_iota(jnp.int32, (IDS, TILE), 1) % IDS
        == lax.broadcasted_iota(jnp.int32, (IDS, TILE), 0)
    )
    loads[0].wait()
    ids = jnp.broadcast_to(id_raw[...].astype(f32), (8, IDS)).astype(bf16)
    id_mine[...] = dot_nn(ids, jnp.where(spread, 1.0, 0.0).astype(bf16))
    id_got[head] = id_mine[...]

    pl.semaphore_wait(
        barrier, head_count - 1 + has_prev.astype(jnp.int32) + has_next.astype(jnp.int32)
    )

    id_copies = [
        pltpu.make_async_remote_copy(
            src_ref=id_mine,
            dst_ref=id_got.at[head],
            send_sem=id_send_sem.at[j],
            recv_sem=id_recv_sem.at[j],
            device_id=device,
            device_id_type=MESH,
        )
        for j, device in enumerate(peers)
    ]
    for copy in id_copies:
        copy.start()

    def to(device, i, src, dst):
        return pltpu.make_async_remote_copy(
            src_ref=src,
            dst_ref=dst,
            send_sem=send_sem.at[i],
            recv_sem=recv_sem.at[i],
            device_id=device,
            device_id_type=MESH,
        )

    send_k = to(nxt, 0, k_hbm, k_prev)
    send_v = to(nxt, 1, v_hbm, v_prev)
    send_id = to(nxt, 2, id_own, id_prev)
    send_gk = to(prv, 3, gk_out, gk_in)
    send_gv = to(prv, 4, gv_out, gv_in)
    pl.when(has_next)(send_k.start)

    def pack_k(k, base):
        a, b, c = parts3(k)
        kc[base : base + 2 * TILE] = lanes(a, a, b, b, c, a)
        kt[:, base : base + 2 * TILE] = rows(*parts2(k.T))

    def pack_v(v, base):
        a, b = parts2(v)
        vc[base : base + 2 * TILE] = lanes(a, a, b, b)
        vt[:, base : base + 2 * TILE] = rows(*parts2(v.T))

    loads[1].wait()
    loads[2].wait()
    pack_k(k_own[...], 2 * TILE)
    pack_v(v_own[...], 2 * TILE)
    loads[3].wait()
    loads[4].wait()

    def q_pack(t, pair):
        a, b, c = (qp[t, pair, :, i * TILE : (i + 1) * TILE] for i in range(3))
        return lanes(a, b, a, b, a, c)

    def g_pack(t, pair):
        g = gp[t, pair]
        return lanes(g, g)

    def own_scores(pair, _):
        columns = pl.ds(pl.multiple_of(pair * 2 * TILE, 2 * TILE), 2 * TILE)
        for t in range(TASKS):
            of_task = slice(t * TILE, (t + 1) * TILE)
            q = qf[of_task, columns] * (SCORE_SCALE * LOG2E)
            qp[t, pair] = lanes(*parts3(rows(q[:, :TILE], q[:, TILE:])))
            g = gf[of_task, columns]
            gp[t, pair] = lanes(*parts2(rows(g[:, :TILE], g[:, TILE:])))
            own = slice(2 * TILE, (3 + t) * TILE)
            kept = slice(t * TILE, (1 + 2 * t) * TILE)
            s_own[pair, kept] = dot_nt(kc[own], q_pack(t, pair))
            dp_own[pair, kept] = dot_nt(vc[own], g_pack(t, pair))
        return 0

    lax.fori_loop(0, PAIRS, own_scores, 0, unroll=True)

    for copy in id_copies:
        copy.wait_recv()
    lane_group = lax.broadcasted_iota(jnp.int32, (8, TILE), 1) // IDS
    for t in range(TASKS):
        row = id_got[4 * t]
        for j in range(1, TILE // IDS):
            row = jnp.where(lane_group == j, id_got[4 * t + j], row)
        id_own[t] = row
    pl.when(has_next)(send_id.start)
    pl.when(has_next)(send_v.start)
    pl.when(has_prev)(send_id.wait_recv)
    id_rows = [id_prev[t] for t in range(TASKS)]
    id_rows += [id_own[t] for t in range(TASKS)]
    wide = [jnp.broadcast_to(r[0:1], (TILE, TILE)) for r in id_rows]
    causal = lax.broadcasted_iota(jnp.int32, (TILE, TILE), 0) <= lax.broadcasted_iota(
        jnp.int32, (TILE, TILE), 1
    )
    for t in range(TASKS):
        for j in range(3):
            allowed = wide[t + j].T == wide[2 + t]
            if j == 2:
                allowed = allowed & causal
            bias[t, j * TILE : (j + 1) * TILE] = jnp.where(allowed, 0.0, NEG)

    pl.when(has_prev)(send_k.wait_recv)
    pack_k(k_prev[...], 0)

    acc_k[...] = jnp.zeros_like(acc_k)
    acc_v[...] = jnp.zeros_like(acc_v)

    def probs(pair, _):
        for t in range(TASKS):
            before = slice(t * TILE, 2 * TILE)
            kept = slice(t * TILE, (1 + 2 * t) * TILE)
            b = bias[t]
            s = rows(dot_nt(kc[before], q_pack(t, pair)), s_own[pair, kept]) + lanes(b, b)
            weights = jnp.exp2(s - jnp.max(s, axis=0, keepdims=True))
            p = weights * (1.0 / jnp.sum(weights, axis=0, keepdims=True))
            pf[t, pair] = p
            high, low = parts2(p)
            p1[t, pair] = high
            p2[t, pair] = low
            g = gp[t, pair]
            ahead = (2 - t) * TILE
            acc_v[before] += dot_nn(lanes(high[:ahead], low[:ahead]), rows(g, g))
        return 0

    lax.fori_loop(0, PAIRS, probs, 0, unroll=True)
    gv_out[...] = acc_v[: 2 * TILE, :TILE] + acc_v[: 2 * TILE, TILE:]
    pl.when(has_prev)(send_gv.start)

    def own_values(pair, _):
        for t in range(TASKS):
            own = slice(2 * TILE, (3 + t) * TILE)
            ahead = (2 - t) * TILE
            g = gp[t, pair]
            acc_v[own] += dot_nn(lanes(p1[t, pair, ahead:], p2[t, pair, ahead:]), rows(g, g))
        return 0

    lax.fori_loop(0, PAIRS, own_values, 0, unroll=True)

    pl.when(has_prev)(send_v.wait_recv)
    pack_v(v_prev[...], 0)

    def grads(pair, _):
        for t in range(TASKS):
            before = slice(t * TILE, 2 * TILE)
            kept = slice(t * TILE, (1 + 2 * t) * TILE)
            dp = rows(dot_nt(vc[before], g_pack(t, pair)), dp_own[pair, kept])
            p = pf[t, pair]
            delta = jnp.sum(p * dp, axis=0, keepdims=True)
            high, low = parts2(p * (dp - delta))
            ds1[t, pair] = high
            ds2[t, pair] = low
            q = qp[t, pair, :, : 2 * TILE]
            ahead = (2 - t) * TILE
            acc_k[before] += dot_nn(lanes(high[:ahead], low[:ahead]), rows(q, q))
        return 0

    lax.fori_loop(0, PAIRS, grads, 0, unroll=True)
    gk_out[...] = (acc_k[: 2 * TILE, :TILE] + acc_k[: 2 * TILE, TILE:]) * (1.0 / LOG2E)
    pl.when(has_prev)(send_gk.start)

    def results(pair, _):
        for t in range(TASKS):
            own = slice(2 * TILE, (3 + t) * TILE)
            ahead = (2 - t) * TILE
            q = qp[t, pair, :, : 2 * TILE]
            acc_k[own] += dot_nn(lanes(ds1[t, pair, ahead:], ds2[t, pair, ahead:]), rows(q, q))
            window = slice(t * TILE, (t + 3) * TILE)
            of_task = slice(t * TILE, (t + 1) * TILE)
            for mat, high, low, out, scale in (
                (vt, p1, p2, o_ref, None),
                (kt, ds1, ds2, dq_ref, SCORE_SCALE),
            ):
                m = mat[:, window]
                both = dot_nn(lanes(m, m), rows(high[t, pair], low[t, pair]))
                x = both[:TILE] + both[TILE:]
                if scale is not None:
                    x = x * scale
                for h in range(2):
                    columns = pl.ds(
                        pl.multiple_of(pair * 2 * TILE + h * TILE, TILE), TILE
                    )
                    out[of_task, columns] = x[:, h * TILE : (h + 1) * TILE].T
        return 0

    lax.fori_loop(0, PAIRS, results, 0, unroll=True)

    pl.when(has_next)(send_gv.wait_recv)
    dv_ref[...] = acc_v[2 * TILE :, :TILE] + acc_v[2 * TILE :, TILE:] + gv_in[...]
    pl.when(has_next)(send_gk.wait_recv)
    dk_ref[...] = (acc_k[2 * TILE :, :TILE] + acc_k[2 * TILE :, TILE:]) * (
        1.0 / LOG2E
    ) + gk_in[...]
    for copy in id_copies:
        copy.wait_send()
    for copy in (send_k, send_v, send_id):
        pl.when(has_next)(copy.wait_send)
    for copy in (send_gk, send_gv):
        pl.when(has_prev)(copy.wait_send)


def place(a, b, c, d, a_out, b_out, c_out, d_out, sem):
    copies = [
        pltpu.make_async_copy(src, dst, sem.at[i])
        for i, (src, dst) in enumerate([(a, a_out), (b, b_out), (c, c_out), (d, d_out)])
    ]
    for copy in copies:
        copy.start()
    for copy in copies:
        copy.wait()


def per_device(queries, keys, values, cotangent, doc_ids):
    tok_count = lax.axis_size("tok")
    head_count = lax.axis_size("head")
    vmem = pl.BlockSpec(memory_space=pltpu.VMEM)
    hbm = pl.BlockSpec(memory_space=pl.ANY)
    own = 2 * TILE
    win = 3 * TILE
    V = pltpu.VMEM
    found = pl.pallas_call(
        functools.partial(kernel, tok_count, head_count),
        out_shape=(
            jax.ShapeDtypeStruct(queries.shape, f32),
            jax.ShapeDtypeStruct(queries.shape, f32),
            jax.ShapeDtypeStruct(keys.shape, f32),
            jax.ShapeDtypeStruct(keys.shape, f32),
        ),
        in_specs=[hbm] * 5,
        out_specs=(vmem, vmem, vmem, vmem),
        scratch_shapes=[
            V(queries.shape, f32),
            V(queries.shape, f32),
            *[V(keys.shape, f32) for _ in range(8)],
            V((1, IDS), jnp.int32),
            V((8, TILE), f32),
            V((head_count, 8, TILE), f32),
            V((TASKS, 8, TILE), f32),
            V((TASKS, 8, TILE), f32),
            V((TASKS, win, TILE), f32),
            V((TASKS, PAIRS, own, 3 * TILE), bf16),
            V((TASKS, PAIRS, own, 2 * TILE), bf16),
            V((2 * own, 6 * TILE), bf16),
            V((2 * own, 4 * TILE), bf16),
            V((2 * TILE, 2 * own), bf16),
            V((2 * TILE, 2 * own), bf16),
            V((PAIRS, win, own), f32),
            V((PAIRS, win, own), f32),
            V((TASKS, PAIRS, win, own), f32),
            *[V((TASKS, PAIRS, win, own), bf16) for _ in range(4)],
            V((2 * own, 2 * TILE), f32),
            V((2 * own, 2 * TILE), f32),
            pltpu.SemaphoreType.DMA((5,)),
            pltpu.SemaphoreType.DMA((5,)),
            pltpu.SemaphoreType.DMA((5,)),
            pltpu.SemaphoreType.DMA((head_count - 1,)),
            pltpu.SemaphoreType.DMA((head_count - 1,)),
        ],
        compiler_params=pltpu.CompilerParams(
            collective_id=0, has_side_effects=True, vmem_limit_bytes=40 * 1024 * 1024
        ),
    )(
        *(
            pltpu.with_memory_space_constraint(x, pltpu.HBM)
            for x in (queries, keys, values, cotangent, doc_ids.reshape(1, IDS))
        )
    )
    return pl.pallas_call(
        place,
        out_shape=tuple(jax.ShapeDtypeStruct(x.shape, f32) for x in found),
        in_specs=[hbm] * 4,
        out_specs=(hbm,) * 4,
        scratch_shapes=[pltpu.SemaphoreType.DMA((4,))],
        compiler_params=pltpu.CompilerParams(vmem_limit_bytes=1024 * 1024),
    )(*found)


def solution(mesh):
    placed = (
        P("tok", "head"),
        P("tok", "head"),
        P("tok", "head"),
        P("tok", "head"),
        P(("tok", "head")),
    )
    return jax.shard_map(
        per_device,
        mesh=mesh,
        in_specs=placed,
        out_specs=(P("tok", "head"), P("tok", "head"), P("tok", "head"), P("tok", "head")),
        check_vma=False,
    )
```

```python
import functools
import math

import jax
import jax.numpy as jnp
from jax import lax
from jax.experimental import pallas as pl
from jax.experimental.pallas import tpu as pltpu
from jax.sharding import PartitionSpec as P

HEAD_DIM = 128
TILE = 128
PAIRS = 4
TASKS = 2
IDS = 32
MESH = pl.DeviceIdType.MESH
SCORE_SCALE = HEAD_DIM**-0.5
LOG2E = math.log2(math.e)
NEG = -1e30

f32 = jnp.float32
bf16 = jnp.bfloat16


def parts2(x):
    high = x.astype(bf16)
    low = (x - high.astype(f32)).astype(bf16)
    return high, low


def parts3(x):
    high = x.astype(bf16)
    rest = x - high.astype(f32)
    mid = rest.astype(bf16)
    low = (rest - mid.astype(f32)).astype(bf16)
    return high, mid, low


def lanes(*xs):
    return jnp.concatenate(xs, axis=1)


def rows(*xs):
    return jnp.concatenate(xs, axis=0)


def dot_nn(a, b):
    return lax.dot_general(a, b, (((1,), (0,)), ((), ())), preferred_element_type=f32)


def dot_nt(a, b):
    return lax.dot_general(a, b, (((1,), (1,)), ((), ())), preferred_element_type=f32)


def kernel(
    tok_count,
    head_count,
    q_hbm,
    k_hbm,
    v_hbm,
    g_hbm,
    ids_hbm,
    o_ref,
    dq_ref,
    dk_ref,
    dv_ref,
    qf,
    gf,
    k_own,
    v_own,
    k_prev,
    v_prev,
    gk_out,
    gv_out,
    gk_in,
    gv_in,
    id_raw,
    id_mine,
    id_got,
    bias,
    qp,
    gp,
    kc,
    vc,
    kt,
    vt,
    s_own,
    dp_own,
    inverse,
    delta,
    pf,
    p1,
    p2,
    ds1,
    ds2,
    acc_k,
    acc_v,
    local_sem,
    send_sem,
    recv_sem,
    id_send_sem,
    id_recv_sem,
    ready_sem,
):
    tok = lax.axis_index("tok")
    head = lax.axis_index("head")
    nxt = (lax.rem(tok + 1, tok_count), head)
    prv = (lax.rem(tok + tok_count - 1, tok_count), head)
    has_prev = tok > 0
    has_next = tok < tok_count - 1

    def rank(h):
        return h + jnp.where((tok == 0) & (h == 0), head_count, 0)

    others = [lax.rem(head + j, head_count) for j in range(1, head_count)]
    mine = rank(head)
    above = [rank(h) > mine for h in others]

    def total(flags):
        return sum(flag.astype(jnp.int32) for flag in flags)

    barrier = pltpu.get_barrier_semaphore()

    def signal(semaphore, device):
        pl.semaphore_signal(semaphore, inc=1, device_id=device, device_id_type=MESH)

    pl.when(has_next)(lambda: signal(barrier, nxt))
    pl.when(has_prev)(lambda: signal(barrier, prv))
    for h, flag in zip(others, above):
        pl.when(flag)(functools.partial(signal, barrier, (tok, h)))

    loads = [
        pltpu.make_async_copy(src, dst, local_sem.at[i])
        for i, (src, dst) in enumerate(
            [(ids_hbm, id_raw), (k_hbm, k_own), (v_hbm, v_own), (q_hbm, qf), (g_hbm, gf)]
        )
    ]
    for load in loads:
        load.start()

    @pl.when(jnp.logical_not(has_prev))
    def _():
        k_prev[...] = jnp.zeros_like(k_prev)
        v_prev[...] = jnp.zeros_like(v_prev)
        for h in range(head_count):
            id_got[head_count + h] = jnp.full_like(id_mine, -1.0)

    @pl.when(jnp.logical_not(has_next))
    def _():
        gk_in[...] = jnp.zeros_like(gk_in)
        gv_in[...] = jnp.zeros_like(gv_in)

    spread = (
        lax.broadcasted_iota(jnp.int32, (IDS, TILE), 1) % IDS
        == lax.broadcasted_iota(jnp.int32, (IDS, TILE), 0)
    )
    loads[0].wait()
    ids = jnp.broadcast_to(id_raw[...].astype(f32), (8, IDS)).astype(bf16)
    id_mine[...] = dot_nn(ids, jnp.where(spread, 1.0, 0.0).astype(bf16))
    id_got[head] = id_mine[...]

    pl.semaphore_wait(barrier, head_count - 1 - total(above) + total([has_next, has_prev]))

    def send_ids(device, i, src, slot):
        return pltpu.make_async_remote_copy(
            src_ref=src,
            dst_ref=id_got.at[slot],
            send_sem=id_send_sem.at[i],
            recv_sem=id_recv_sem.at[i],
            device_id=device,
            device_id_type=MESH,
        )

    slot = head_count + head
    ids_next = send_ids(nxt, 0, id_mine, slot)
    ids_beside = [send_ids((tok, h), 1 + j, id_mine, head) for j, h in enumerate(others)]
    ids_on = [
        send_ids((tok, h), head_count + j, id_got.at[slot], slot) for j, h in enumerate(others)
    ]

    def to(device, i, src, dst):
        return pltpu.make_async_remote_copy(
            src_ref=src,
            dst_ref=dst,
            send_sem=send_sem.at[i],
            recv_sem=recv_sem.at[i],
            device_id=device,
            device_id_type=MESH,
        )

    send_k = to(nxt, 0, k_hbm, k_prev)
    send_v = to(nxt, 1, v_hbm, v_prev)
    halves = [pl.ds(t * TILE, TILE) for t in range(TASKS)]
    send_gv = [to(prv, 2 + t, gv_out.at[r], gv_in.at[r]) for t, r in enumerate(halves)]
    send_gk = [to(prv, 4 + t, gk_out.at[r], gk_in.at[r]) for t, r in enumerate(halves)]

    @pl.when(has_next)
    def _():
        ids_next.start()
        send_k.start()
        send_v.start()

    for h, copy, flag in zip(others, ids_beside, above):

        @pl.when(jnp.logical_not(flag))
        def _():
            signal(ready_sem, (tok, h))
            copy.start()

    def pack_k(k, base):
        a, b, c = parts3(k)
        kc[base : base + 2 * TILE] = lanes(a, a, b, b, c, a)
        kt[:, base : base + 2 * TILE] = rows(*parts2(k.T))

    def pack_v(v, base):
        a, b = parts2(v)
        vc[base : base + 2 * TILE] = lanes(a, a, b, b)
        vt[:, base : base + 2 * TILE] = rows(*parts2(v.T))

    loads[1].wait()
    loads[2].wait()
    pack_k(k_own[...], 2 * TILE)
    pack_v(v_own[...], 2 * TILE)
    loads[3].wait()
    loads[4].wait()

    waiting = total(above)

    @pl.when(waiting > 0)
    def _():
        pl.semaphore_wait(ready_sem, waiting)

    for copy, flag in zip(ids_beside, above):
        pl.when(flag)(copy.start)

    def q_pack(t, pair):
        a, b, c = (qp[t, pair, :, i * TILE : (i + 1) * TILE] for i in range(3))
        return lanes(a, b, a, b, a, c)

    def g_pack(t, pair):
        g = gp[t, pair]
        return lanes(g, g)

    def own_scores(pair, _):
        columns = pl.ds(pl.multiple_of(pair * 2 * TILE, 2 * TILE), 2 * TILE)
        for t in range(TASKS):
            of_task = slice(t * TILE, (t + 1) * TILE)
            q = qf[of_task, columns] * (SCORE_SCALE * LOG2E)
            qp[t, pair] = lanes(*parts3(rows(q[:, :TILE], q[:, TILE:])))
            g = gf[of_task, columns]
            gp[t, pair] = lanes(*parts2(rows(g[:, :TILE], g[:, TILE:])))
            own = slice(2 * TILE, (3 + t) * TILE)
            kept = slice(t * TILE, (1 + 2 * t) * TILE)
            s_own[pair, kept] = dot_nt(kc[own], q_pack(t, pair))
            dp_own[pair, kept] = dot_nt(vc[own], g_pack(t, pair))
        return 0

    lax.fori_loop(0, PAIRS, own_scores, 0, unroll=True)

    @pl.when(has_prev)
    def _():
        ids_next.wait_recv()
        for copy in ids_on:
            copy.start()


    pl.when(has_prev)(send_k.wait_recv)
    pack_k(k_prev[...], 0)

    acc_k[...] = jnp.zeros_like(acc_k)
    acc_v[...] = jnp.zeros_like(acc_v)

    def earlier_scores(pair, _):
        for t in range(TASKS):
            before = slice(t * TILE, 2 * TILE)
            pf[t, pair, : (2 - t) * TILE] = dot_nt(kc[before], q_pack(t, pair))
        return 0

    lax.fori_loop(0, PAIRS, earlier_scores, 0, unroll=True)

    for copy in ids_beside:
        copy.wait_recv()

    @pl.when(has_prev)
    def _():
        for copy in ids_on:
            copy.wait_recv()

    lane_group = lax.broadcasted_iota(jnp.int32, (8, TILE), 1) // IDS
    per_tile = TILE // IDS
    wide = []
    for first in (head_count, head_count + per_tile, 0, per_tile):
        row = id_got[first]
        for j in range(1, per_tile):
            row = jnp.where(lane_group == j, id_got[first + j], row)
        wide.append(jnp.broadcast_to(row[0:1], (TILE, TILE)))
    causal = lax.broadcasted_iota(jnp.int32, (TILE, TILE), 0) <= lax.broadcasted_iota(
        jnp.int32, (TILE, TILE), 1
    )
    for t in range(TASKS):
        for j in range(3):
            allowed = wide[t + j].T == wide[2 + t]
            if j == 2:
                allowed = allowed & causal
            bias[t, j * TILE : (j + 1) * TILE] = jnp.where(allowed, 0.0, NEG)

    def probs(t, pair, _):
        before = slice(t * TILE, 2 * TILE)
        kept = slice(t * TILE, (1 + 2 * t) * TILE)
        ahead = (2 - t) * TILE
        b = bias[t]
        s_prev = pf[t, pair, :ahead] + lanes(b[:ahead], b[:ahead])
        s_here = s_own[pair, kept] + lanes(b[ahead:], b[ahead:])
        top = jnp.maximum(
            jnp.max(s_prev, axis=0, keepdims=True), jnp.max(s_here, axis=0, keepdims=True)
        )
        w_prev = jnp.exp2(s_prev - top)
        w_here = jnp.exp2(s_here - top)
        s_own[pair, kept] = w_here
        inv = 1.0 / (
            jnp.sum(w_prev, axis=0, keepdims=True) + jnp.sum(w_here, axis=0, keepdims=True)
        )
        inverse[t, pair] = inv
        p = w_prev * inv
        pf[t, pair, :ahead] = p
        high, low = parts2(p)
        p1[t, pair, :ahead] = high
        p2[t, pair, :ahead] = low
        g = gp[t, pair]
        acc_v[before] += dot_nn(lanes(high, low), rows(g, g))
        return 0

    for t in range(TASKS):
        lax.fori_loop(0, PAIRS, functools.partial(probs, t), 0, unroll=True)
        tile = slice(t * TILE, (t + 1) * TILE)
        gv_out[tile] = acc_v[tile, :TILE] + acc_v[tile, TILE:]
        pl.when(has_prev)(send_gv[t].start)

    pl.when(has_prev)(send_v.wait_recv)
    pack_v(v_prev[...], 0)

    def grads(t, pair, _):
        before = slice(t * TILE, 2 * TILE)
        kept = slice(t * TILE, (1 + 2 * t) * TILE)
        ahead = (2 - t) * TILE
        of_own = jnp.sum(s_own[pair, kept] * dp_own[pair, kept], axis=0, keepdims=True)
        dp = dot_nt(vc[before], g_pack(t, pair))
        p = pf[t, pair, :ahead]
        row_delta = of_own * inverse[t, pair] + jnp.sum(p * dp, axis=0, keepdims=True)
        delta[t, pair] = row_delta
        high, low = parts2(p * (dp - row_delta))
        ds1[t, pair, :ahead] = high
        ds2[t, pair, :ahead] = low
        q = qp[t, pair, :, : 2 * TILE]
        acc_k[before] += dot_nn(lanes(high, low), rows(q, q))
        return 0

    for t in range(TASKS):
        lax.fori_loop(0, PAIRS, functools.partial(grads, t), 0, unroll=True)
        tile = slice(t * TILE, (t + 1) * TILE)
        gk_out[tile] = (acc_k[tile, :TILE] + acc_k[tile, TILE:]) * (1.0 / LOG2E)
        pl.when(has_prev)(send_gk[t].start)

    def results(pair, _):
        for t in range(TASKS):
            own = slice(2 * TILE, (3 + t) * TILE)
            kept = slice(t * TILE, (1 + 2 * t) * TILE)
            ahead = (2 - t) * TILE
            p = s_own[pair, kept] * inverse[t, pair]
            p_high, p_low = parts2(p)
            d_high, d_low = parts2(p * (dp_own[pair, kept] - delta[t, pair]))
            g = gp[t, pair]
            acc_v[own] += dot_nn(lanes(p_high, p_low), rows(g, g))
            q = qp[t, pair, :, : 2 * TILE]
            acc_k[own] += dot_nn(lanes(d_high, d_low), rows(q, q))
            window = slice(t * TILE, (t + 3) * TILE)
            of_task = slice(t * TILE, (t + 1) * TILE)
            for mat, first, second, high, low, out, scale in (
                (vt, p1, p2, p_high, p_low, o_ref, None),
                (kt, ds1, ds2, d_high, d_low, dq_ref, SCORE_SCALE),
            ):
                m = mat[:, window]
                both = dot_nn(
                    lanes(m, m),
                    rows(first[t, pair, :ahead], high, second[t, pair, :ahead], low),
                )
                x = both[:TILE] + both[TILE:]
                if scale is not None:
                    x = x * scale
                for h in range(2):
                    columns = pl.ds(
                        pl.multiple_of(pair * 2 * TILE + h * TILE, TILE), TILE
                    )
                    out[of_task, columns] = x[:, h * TILE : (h + 1) * TILE].T
        return 0

    lax.fori_loop(0, PAIRS, results, 0, unroll=True)

    dv_own = acc_v[2 * TILE :, :TILE] + acc_v[2 * TILE :, TILE:]
    dk_own = (acc_k[2 * TILE :, :TILE] + acc_k[2 * TILE :, TILE:]) * (1.0 / LOG2E)
    for own, sent, got, out in ((dv_own, send_gv, gv_in, dv_ref), (dk_own, send_gk, gk_in, dk_ref)):
        for t in range(TASKS):
            tile = slice(t * TILE, (t + 1) * TILE)
            pl.when(has_next)(sent[t].wait_recv)
            out[tile] = own[tile] + got[tile]
    for copy in ids_beside:
        copy.wait_send()
    for copy in (ids_next, send_k, send_v):
        pl.when(has_next)(copy.wait_send)
    for copy in (*ids_on, *send_gk, *send_gv):
        pl.when(has_prev)(copy.wait_send)


def place(a, b, c, d, a_out, b_out, c_out, d_out, sem):
    copies = [
        pltpu.make_async_copy(src, dst, sem.at[i])
        for i, (src, dst) in enumerate([(a, a_out), (b, b_out), (c, c_out), (d, d_out)])
    ]
    for copy in copies:
        copy.start()
    for copy in copies:
        copy.wait()


def per_device(queries, keys, values, cotangent, doc_ids):
    tok_count = lax.axis_size("tok")
    head_count = lax.axis_size("head")
    vmem = pl.BlockSpec(memory_space=pltpu.VMEM)
    hbm = pl.BlockSpec(memory_space=pl.ANY)
    own = 2 * TILE
    win = 3 * TILE
    V = pltpu.VMEM
    found = pl.pallas_call(
        functools.partial(kernel, tok_count, head_count),
        out_shape=(
            jax.ShapeDtypeStruct(queries.shape, f32),
            jax.ShapeDtypeStruct(queries.shape, f32),
            jax.ShapeDtypeStruct(keys.shape, f32),
            jax.ShapeDtypeStruct(keys.shape, f32),
        ),
        in_specs=[hbm] * 5,
        out_specs=(vmem, vmem, vmem, vmem),
        scratch_shapes=[
            V(queries.shape, f32),
            V(queries.shape, f32),
            *[V(keys.shape, f32) for _ in range(8)],
            V((1, IDS), jnp.int32),
            V((8, TILE), f32),
            V((2 * head_count, 8, TILE), f32),
            V((TASKS, win, TILE), f32),
            V((TASKS, PAIRS, own, 3 * TILE), bf16),
            V((TASKS, PAIRS, own, 2 * TILE), bf16),
            V((2 * own, 6 * TILE), bf16),
            V((2 * own, 4 * TILE), bf16),
            V((2 * TILE, 2 * own), bf16),
            V((2 * TILE, 2 * own), bf16),
            V((PAIRS, win, own), f32),
            V((PAIRS, win, own), f32),
            V((TASKS, PAIRS, 1, own), f32),
            V((TASKS, PAIRS, 1, own), f32),
            V((TASKS, PAIRS, own, own), f32),
            *[V((TASKS, PAIRS, own, own), bf16) for _ in range(4)],
            V((2 * own, 2 * TILE), f32),
            V((2 * own, 2 * TILE), f32),
            pltpu.SemaphoreType.DMA((5,)),
            pltpu.SemaphoreType.DMA((6,)),
            pltpu.SemaphoreType.DMA((6,)),
            pltpu.SemaphoreType.DMA((2 * head_count,)),
            pltpu.SemaphoreType.DMA((2 * head_count,)),
            pltpu.SemaphoreType.REGULAR,
        ],
        compiler_params=pltpu.CompilerParams(
            collective_id=0, has_side_effects=True, vmem_limit_bytes=40 * 1024 * 1024
        ),
    )(
        *(
            pltpu.with_memory_space_constraint(x, pltpu.HBM)
            for x in (queries, keys, values, cotangent, doc_ids.reshape(1, IDS))
        )
    )
    return pl.pallas_call(
        place,
        out_shape=tuple(jax.ShapeDtypeStruct(x.shape, f32) for x in found),
        in_specs=[hbm] * 4,
        out_specs=(hbm,) * 4,
        scratch_shapes=[pltpu.SemaphoreType.DMA((4,))],
        compiler_params=pltpu.CompilerParams(vmem_limit_bytes=1024 * 1024),
    )(*found)


def solution(mesh):
    placed = (
        P("tok", "head"),
        P("tok", "head"),
        P("tok", "head"),
        P("tok", "head"),
        P(("tok", "head")),
    )
    return jax.shard_map(
        per_device,
        mesh=mesh,
        in_specs=placed,
        out_specs=(P("tok", "head"), P("tok", "head"), P("tok", "head"), P("tok", "head")),
        check_vma=False,
    )
```

```python
import functools
import math

import jax
import jax.numpy as jnp
from jax import lax
from jax.experimental import pallas as pl
from jax.experimental.pallas import tpu as pltpu
from jax.sharding import PartitionSpec as P

HEAD_DIM = 128
TILE = 128
PAIRS = 4
TASKS = 2
IDS = 32
MESH = pl.DeviceIdType.MESH
SCORE_SCALE = HEAD_DIM**-0.5
LOG2E = math.log2(math.e)
NEG = -1e30

f32 = jnp.float32
bf16 = jnp.bfloat16


def parts2(x):
    high = x.astype(bf16)
    low = (x - high.astype(f32)).astype(bf16)
    return high, low


def parts3(x):
    high = x.astype(bf16)
    rest = x - high.astype(f32)
    mid = rest.astype(bf16)
    low = (rest - mid.astype(f32)).astype(bf16)
    return high, mid, low


def lanes(*xs):
    return jnp.concatenate(xs, axis=1)


def rows(*xs):
    return jnp.concatenate(xs, axis=0)


def dot_nn(a, b):
    return lax.dot_general(a, b, (((1,), (0,)), ((), ())), preferred_element_type=f32)


def dot_nt(a, b):
    return lax.dot_general(a, b, (((1,), (1,)), ((), ())), preferred_element_type=f32)


def kernel(
    tok_count,
    head_count,
    q_hbm,
    k_hbm,
    v_hbm,
    g_hbm,
    ids_hbm,
    o_ref,
    dq_ref,
    dk_ref,
    dv_ref,
    qf,
    gf,
    k_own,
    v_own,
    k_prev,
    v_prev,
    gk_out,
    gv_out,
    gk_in,
    gv_in,
    id_raw,
    id_mine,
    id_got,
    bias,
    qp,
    gp,
    kc,
    vc,
    kt,
    vt,
    s_own,
    dp_own,
    own_top,
    own_sum,
    own_dot,
    inverse,
    delta,
    pf,
    p1,
    p2,
    ds1,
    ds2,
    acc_k,
    acc_v,
    local_sem,
    send_sem,
    recv_sem,
    id_send_sem,
    id_recv_sem,
    ready_sem,
):
    tok = lax.axis_index("tok")
    head = lax.axis_index("head")
    nxt = (lax.rem(tok + 1, tok_count), head)
    prv = (lax.rem(tok + tok_count - 1, tok_count), head)
    has_prev = tok > 0
    has_next = tok < tok_count - 1

    def rank(h):
        return h + jnp.where((tok == 0) & (h == 0), head_count, 0)

    others = [lax.rem(head + j, head_count) for j in range(1, head_count)]
    mine = rank(head)
    above = [rank(h) > mine for h in others]
    earlier_rank = head + jnp.where((tok == 1) & (head == 0), head_count, 0)
    straight = [has_next & (h < mine) for h in others]
    greeted = [has_prev & ((h > head) | ((tok == 1) & (h == 0))) for h in others]
    relayed = [has_prev & (h > earlier_rank) for h in others]

    def total(flags):
        return sum(flag.astype(jnp.int32) for flag in flags)

    barrier = pltpu.get_barrier_semaphore()

    def signal(semaphore, device):
        pl.semaphore_signal(semaphore, inc=1, device_id=device, device_id_type=MESH)

    pl.when(has_next)(lambda: signal(barrier, nxt))
    pl.when(has_prev)(lambda: signal(barrier, prv))
    for h, flag, flag_prev in zip(others, above, greeted):
        pl.when(flag_prev)(functools.partial(signal, barrier, (prv[0], h)))
        pl.when(flag)(functools.partial(signal, barrier, (tok, h)))

    loads = [
        pltpu.make_async_copy(src, dst, local_sem.at[i])
        for i, (src, dst) in enumerate(
            [(ids_hbm, id_raw), (k_hbm, k_own), (v_hbm, v_own), (q_hbm, qf), (g_hbm, gf)]
        )
    ]
    for load in loads:
        load.start()

    @pl.when(jnp.logical_not(has_prev))
    def _():
        k_prev[...] = jnp.zeros_like(k_prev)
        v_prev[...] = jnp.zeros_like(v_prev)
        for h in range(head_count):
            id_got[head_count + h] = jnp.full_like(id_mine, -1.0)

    @pl.when(jnp.logical_not(has_next))
    def _():
        gk_in[...] = jnp.zeros_like(gk_in)
        gv_in[...] = jnp.zeros_like(gv_in)

    spread = (
        lax.broadcasted_iota(jnp.int32, (IDS, TILE), 1) % IDS
        == lax.broadcasted_iota(jnp.int32, (IDS, TILE), 0)
    )
    loads[0].wait()
    ids = jnp.broadcast_to(id_raw[...].astype(f32), (8, IDS)).astype(bf16)
    id_mine[...] = dot_nn(ids, jnp.where(spread, 1.0, 0.0).astype(bf16))
    id_got[head] = id_mine[...]

    pl.semaphore_wait(barrier, head_count - 1 - total(above) + total([has_next, has_prev, *straight]))

    def send_ids(device, i, src, slot, sent=None):
        return pltpu.make_async_remote_copy(
            src_ref=src,
            dst_ref=id_got.at[slot],
            send_sem=id_send_sem.at[i if sent is None else sent],
            recv_sem=id_recv_sem.at[i],
            device_id=device,
            device_id_type=MESH,
        )

    slot = head_count + head
    ids_next = send_ids(nxt, 0, id_mine, slot)
    ids_beside = [send_ids((tok, h), 1 + j, id_mine, head) for j, h in enumerate(others)]
    ids_straight = [
        send_ids((nxt[0], h), head_count + j, id_mine, slot, 2 * head_count + j)
        for j, h in enumerate(others)
    ]
    ids_on = [
        send_ids((tok, h), head_count + j, id_got.at[slot], slot) for j, h in enumerate(others)
    ]

    def to(device, i, src, dst):
        return pltpu.make_async_remote_copy(
            src_ref=src,
            dst_ref=dst,
            send_sem=send_sem.at[i],
            recv_sem=recv_sem.at[i],
            device_id=device,
            device_id_type=MESH,
        )

    send_k = to(nxt, 0, k_hbm, k_prev)
    send_v = to(nxt, 1, v_hbm, v_prev)
    halves = [pl.ds(t * TILE, TILE) for t in range(TASKS)]
    send_gv = [to(prv, 2 + t, gv_out.at[r], gv_in.at[r]) for t, r in enumerate(halves)]
    send_gk = [to(prv, 4 + t, gk_out.at[r], gk_in.at[r]) for t, r in enumerate(halves)]

    @pl.when(has_next)
    def _():
        ids_next.start()
        for copy, flag in zip(ids_straight, straight):
            pl.when(flag)(copy.start)
        send_k.start()
        send_v.start()

    for h, copy, flag in zip(others, ids_beside, above):

        @pl.when(jnp.logical_not(flag))
        def _():
            signal(ready_sem, (tok, h))
            copy.start()

    def pack_k(k, base):
        a, b, c = parts3(k)
        kc[base : base + 2 * TILE] = lanes(a, a, b, b, c, a)

    def pack_v(v, base):
        a, b = parts2(v)
        vc[base : base + 2 * TILE] = lanes(a, a, b, b)

    def turn(k, v, base):
        kt[:, base : base + 2 * TILE] = rows(*parts2(k.T))
        vt[:, base : base + 2 * TILE] = rows(*parts2(v.T))

    loads[1].wait()
    loads[2].wait()
    pack_k(k_own[...], 2 * TILE)
    pack_v(v_own[...], 2 * TILE)
    turn(k_own[...], v_own[...], 2 * TILE)
    loads[3].wait()
    loads[4].wait()

    waiting = total(above)

    @pl.when(waiting > 0)
    def _():
        pl.semaphore_wait(ready_sem, waiting)

    for copy, flag in zip(ids_beside, above):
        pl.when(flag)(copy.start)

    def q_pack(t, pair):
        a, b, c = (qp[t, pair, :, i * TILE : (i + 1) * TILE] for i in range(3))
        return lanes(a, b, a, b, a, c)

    def g_pack(t, pair):
        g = gp[t, pair]
        return lanes(g, g)

    def own_scores(pair, _):
        columns = pl.ds(pl.multiple_of(pair * 2 * TILE, 2 * TILE), 2 * TILE)
        for t in range(TASKS):
            of_task = slice(t * TILE, (t + 1) * TILE)
            q = qf[of_task, columns] * (SCORE_SCALE * LOG2E)
            qp[t, pair] = lanes(*parts3(rows(q[:, :TILE], q[:, TILE:])))
            g = gf[of_task, columns]
            gp[t, pair] = lanes(*parts2(rows(g[:, :TILE], g[:, TILE:])))
            own = slice(2 * TILE, (3 + t) * TILE)
            kept = slice(t * TILE, (1 + 2 * t) * TILE)
            s_own[pair, kept] = dot_nt(kc[own], q_pack(t, pair))
            dp_own[pair, kept] = dot_nt(vc[own], g_pack(t, pair))
        return 0

    lax.fori_loop(0, PAIRS, own_scores, 0, unroll=True)

    @pl.when(has_prev)
    def _():
        ids_next.wait_recv()
        for copy, flag in zip(ids_on, relayed):
            pl.when(flag)(copy.start)


    lane_group = lax.broadcasted_iota(jnp.int32, (8, TILE), 1) // IDS
    per_tile = TILE // IDS

    def id_row(first):
        row = id_got[first]
        for j in range(1, per_tile):
            row = jnp.where(lane_group == j, id_got[first + j], row)
        return jnp.broadcast_to(row[0:1], (TILE, TILE))

    for copy in ids_beside:
        copy.wait_recv()
    of_queries = [id_row(0), id_row(per_tile)]
    causal = lax.broadcasted_iota(jnp.int32, (TILE, TILE), 0) <= lax.broadcasted_iota(
        jnp.int32, (TILE, TILE), 1
    )

    def set_bias(t, j, allowed):
        bias[t, j * TILE : (j + 1) * TILE] = jnp.where(allowed, 0.0, NEG)

    for t in range(TASKS):
        set_bias(t, 2, (of_queries[t].T == of_queries[t]) & causal)
    set_bias(1, 1, of_queries[0].T == of_queries[1])

    def own_weights(pair, _):
        for t in range(TASKS):
            kept = slice(t * TILE, (1 + 2 * t) * TILE)
            b = bias[t, (2 - t) * TILE :]
            s = s_own[pair, kept] + lanes(b, b)
            top = jnp.max(s, axis=0, keepdims=True)
            w = jnp.exp2(s - top)
            s_own[pair, kept] = w
            own_top[t, pair] = top
            own_sum[t, pair] = jnp.sum(w, axis=0, keepdims=True)
            own_dot[t, pair] = jnp.sum(w * dp_own[pair, kept], axis=0, keepdims=True)
        return 0

    lax.fori_loop(0, PAIRS, own_weights, 0, unroll=True)

    pl.when(has_prev)(send_k.wait_recv)
    pack_k(k_prev[...], 0)

    acc_k[...] = jnp.zeros_like(acc_k)
    acc_v[...] = jnp.zeros_like(acc_v)

    def earlier_scores(pair, _):
        for t in range(TASKS):
            before = slice(t * TILE, 2 * TILE)
            pf[t, pair, : (2 - t) * TILE] = dot_nt(kc[before], q_pack(t, pair))
        return 0

    lax.fori_loop(0, PAIRS, earlier_scores, 0, unroll=True)

    @pl.when(has_prev)
    def _():
        for copy in ids_on:
            copy.wait_recv()

    of_keys = [id_row(head_count).T, id_row(head_count + per_tile).T]
    set_bias(0, 0, of_keys[0] == of_queries[0])
    set_bias(0, 1, of_keys[1] == of_queries[0])
    set_bias(1, 0, of_keys[1] == of_queries[1])

    def probs(t, pair, _):
        before = slice(t * TILE, 2 * TILE)
        kept = slice(t * TILE, (1 + 2 * t) * TILE)
        ahead = (2 - t) * TILE
        b = bias[t, :ahead]
        s_prev = pf[t, pair, :ahead] + lanes(b, b)
        top = jnp.maximum(own_top[t, pair], jnp.max(s_prev, axis=0, keepdims=True))
        w_prev = jnp.exp2(s_prev - top)
        shrink = jnp.exp2(own_top[t, pair] - top)
        inv = 1.0 / (jnp.sum(w_prev, axis=0, keepdims=True) + own_sum[t, pair] * shrink)
        inverse[t, pair] = inv * shrink
        p = w_prev * inv
        pf[t, pair, :ahead] = p
        high, low = parts2(p)
        p1[t, pair, :ahead] = high
        p2[t, pair, :ahead] = low
        g = gp[t, pair]
        acc_v[before] += dot_nn(lanes(high, low), rows(g, g))
        return 0

    for t in range(TASKS):
        lax.fori_loop(0, PAIRS, functools.partial(probs, t), 0, unroll=True)
        tile = slice(t * TILE, (t + 1) * TILE)
        gv_out[tile] = acc_v[tile, :TILE] + acc_v[tile, TILE:]
        pl.when(has_prev)(send_gv[t].start)

    pl.when(has_prev)(send_v.wait_recv)
    pack_v(v_prev[...], 0)

    def grads(t, pair, _):
        before = slice(t * TILE, 2 * TILE)
        kept = slice(t * TILE, (1 + 2 * t) * TILE)
        ahead = (2 - t) * TILE
        dp = dot_nt(vc[before], g_pack(t, pair))
        p = pf[t, pair, :ahead]
        row_delta = own_dot[t, pair] * inverse[t, pair] + jnp.sum(p * dp, axis=0, keepdims=True)
        delta[t, pair] = row_delta
        high, low = parts2(p * (dp - row_delta))
        ds1[t, pair, :ahead] = high
        ds2[t, pair, :ahead] = low
        q = qp[t, pair, :, : 2 * TILE]
        acc_k[before] += dot_nn(lanes(high, low), rows(q, q))
        return 0

    for t in range(TASKS):
        lax.fori_loop(0, PAIRS, functools.partial(grads, t), 0, unroll=True)
        tile = slice(t * TILE, (t + 1) * TILE)
        gk_out[tile] = (acc_k[tile, :TILE] + acc_k[tile, TILE:]) * (1.0 / LOG2E)
        pl.when(has_prev)(send_gk[t].start)

    turn(k_prev[...], v_prev[...], 0)

    def results(pair, _):
        for t in range(TASKS):
            own = slice(2 * TILE, (3 + t) * TILE)
            kept = slice(t * TILE, (1 + 2 * t) * TILE)
            ahead = (2 - t) * TILE
            p = s_own[pair, kept] * inverse[t, pair]
            p_high, p_low = parts2(p)
            d_high, d_low = parts2(p * (dp_own[pair, kept] - delta[t, pair]))
            g = gp[t, pair]
            acc_v[own] += dot_nn(lanes(p_high, p_low), rows(g, g))
            q = qp[t, pair, :, : 2 * TILE]
            acc_k[own] += dot_nn(lanes(d_high, d_low), rows(q, q))
            window = slice(t * TILE, (t + 3) * TILE)
            of_task = slice(t * TILE, (t + 1) * TILE)
            for mat, first, second, high, low, out, scale in (
                (vt, p1, p2, p_high, p_low, o_ref, None),
                (kt, ds1, ds2, d_high, d_low, dq_ref, SCORE_SCALE),
            ):
                m = mat[:, window]
                both = dot_nn(
                    lanes(m, m),
                    rows(first[t, pair, :ahead], high, second[t, pair, :ahead], low),
                )
                x = both[:TILE] + both[TILE:]
                if scale is not None:
                    x = x * scale
                for h in range(2):
                    columns = pl.ds(
                        pl.multiple_of(pair * 2 * TILE + h * TILE, TILE), TILE
                    )
                    out[of_task, columns] = x[:, h * TILE : (h + 1) * TILE].T
        return 0

    lax.fori_loop(0, PAIRS, results, 0, unroll=True)

    dv_own = acc_v[2 * TILE :, :TILE] + acc_v[2 * TILE :, TILE:]
    dk_own = (acc_k[2 * TILE :, :TILE] + acc_k[2 * TILE :, TILE:]) * (1.0 / LOG2E)
    for own, sent, got, out in ((dv_own, send_gv, gv_in, dv_ref), (dk_own, send_gk, gk_in, dk_ref)):
        for t in range(TASKS):
            tile = slice(t * TILE, (t + 1) * TILE)
            pl.when(has_next)(sent[t].wait_recv)
            out[tile] = own[tile] + got[tile]
    for copy in ids_beside:
        copy.wait_send()
    for copy in (ids_next, send_k, send_v):
        pl.when(has_next)(copy.wait_send)
    for copy in (*send_gk, *send_gv):
        pl.when(has_prev)(copy.wait_send)
    for copy, flag in zip((*ids_on, *ids_straight), (*relayed, *straight)):
        pl.when(flag)(copy.wait_send)


def place(a, b, c, d, a_out, b_out, c_out, d_out, sem):
    copies = [
        pltpu.make_async_copy(src, dst, sem.at[i])
        for i, (src, dst) in enumerate([(a, a_out), (b, b_out), (c, c_out), (d, d_out)])
    ]
    for copy in copies:
        copy.start()
    for copy in copies:
        copy.wait()


def per_device(queries, keys, values, cotangent, doc_ids):
    tok_count = lax.axis_size("tok")
    head_count = lax.axis_size("head")
    vmem = pl.BlockSpec(memory_space=pltpu.VMEM)
    hbm = pl.BlockSpec(memory_space=pl.ANY)
    own = 2 * TILE
    win = 3 * TILE
    V = pltpu.VMEM
    found = pl.pallas_call(
        functools.partial(kernel, tok_count, head_count),
        out_shape=(
            jax.ShapeDtypeStruct(queries.shape, f32),
            jax.ShapeDtypeStruct(queries.shape, f32),
            jax.ShapeDtypeStruct(keys.shape, f32),
            jax.ShapeDtypeStruct(keys.shape, f32),
        ),
        in_specs=[hbm] * 5,
        out_specs=(vmem, vmem, vmem, vmem),
        scratch_shapes=[
            V(queries.shape, f32),
            V(queries.shape, f32),
            *[V(keys.shape, f32) for _ in range(8)],
            V((1, IDS), jnp.int32),
            V((8, TILE), f32),
            V((2 * head_count, 8, TILE), f32),
            V((TASKS, win, TILE), f32),
            V((TASKS, PAIRS, own, 3 * TILE), bf16),
            V((TASKS, PAIRS, own, 2 * TILE), bf16),
            V((2 * own, 6 * TILE), bf16),
            V((2 * own, 4 * TILE), bf16),
            V((2 * TILE, 2 * own), bf16),
            V((2 * TILE, 2 * own), bf16),
            V((PAIRS, win, own), f32),
            V((PAIRS, win, own), f32),
            *[V((TASKS, PAIRS, 1, own), f32) for _ in range(5)],
            V((TASKS, PAIRS, own, own), f32),
            *[V((TASKS, PAIRS, own, own), bf16) for _ in range(4)],
            V((2 * own, 2 * TILE), f32),
            V((2 * own, 2 * TILE), f32),
            pltpu.SemaphoreType.DMA((5,)),
            pltpu.SemaphoreType.DMA((6,)),
            pltpu.SemaphoreType.DMA((6,)),
            pltpu.SemaphoreType.DMA((3 * head_count,)),
            pltpu.SemaphoreType.DMA((2 * head_count,)),
            pltpu.SemaphoreType.REGULAR,
        ],
        compiler_params=pltpu.CompilerParams(
            collective_id=0, has_side_effects=True, vmem_limit_bytes=40 * 1024 * 1024
        ),
    )(
        *(
            pltpu.with_memory_space_constraint(x, pltpu.HBM)
            for x in (queries, keys, values, cotangent, doc_ids.reshape(1, IDS))
        )
    )
    return pl.pallas_call(
        place,
        out_shape=tuple(jax.ShapeDtypeStruct(x.shape, f32) for x in found),
        in_specs=[hbm] * 4,
        out_specs=(hbm,) * 4,
        scratch_shapes=[pltpu.SemaphoreType.DMA((4,))],
        compiler_params=pltpu.CompilerParams(vmem_limit_bytes=1024 * 1024),
    )(*found)


def solution(mesh):
    placed = (
        P("tok", "head"),
        P("tok", "head"),
        P("tok", "head"),
        P("tok", "head"),
        P(("tok", "head")),
    )
    return jax.shard_map(
        per_device,
        mesh=mesh,
        in_specs=placed,
        out_specs=(P("tok", "head"), P("tok", "head"), P("tok", "head"), P("tok", "head")),
        check_vma=False,
    )
```

```python
import functools
import math

import jax
import jax.numpy as jnp
from jax import lax
from jax.experimental import pallas as pl
from jax.experimental.pallas import tpu as pltpu
from jax.sharding import PartitionSpec as P

HEAD_DIM = 128
TILE = 128
PAIRS = 4
TASKS = 2
IDS = 32
MESH = pl.DeviceIdType.MESH
SCORE_SCALE = HEAD_DIM**-0.5
LOG2E = math.log2(math.e)
NEG = -1e30

f32 = jnp.float32
bf16 = jnp.bfloat16


def parts2(x):
    high = x.astype(bf16)
    low = (x - high.astype(f32)).astype(bf16)
    return high, low


def parts3(x):
    high = x.astype(bf16)
    rest = x - high.astype(f32)
    mid = rest.astype(bf16)
    low = (rest - mid.astype(f32)).astype(bf16)
    return high, mid, low


def lanes(*xs):
    return jnp.concatenate(xs, axis=1)


def rows(*xs):
    return jnp.concatenate(xs, axis=0)


def dot_nn(a, b):
    return lax.dot_general(a, b, (((1,), (0,)), ((), ())), preferred_element_type=f32)


def dot_nt(a, b):
    return lax.dot_general(a, b, (((1,), (1,)), ((), ())), preferred_element_type=f32)


def kernel(
    tok_count,
    head_count,
    q_hbm,
    k_hbm,
    v_hbm,
    g_hbm,
    ids_hbm,
    o_ref,
    dq_ref,
    dk_ref,
    dv_ref,
    qf,
    gf,
    k_own,
    v_own,
    k_prev,
    v_prev,
    gk_out,
    gv_out,
    gk_in,
    gv_in,
    id_raw,
    id_mine,
    id_got,
    bias,
    qp,
    gp,
    kc,
    vc,
    kt,
    vt,
    s_own,
    dp_own,
    own_top,
    own_sum,
    own_dot,
    inverse,
    delta,
    pf,
    p1,
    p2,
    ds1,
    ds2,
    acc_k,
    acc_v,
    local_sem,
    send_sem,
    recv_sem,
    id_send_sem,
    id_recv_sem,
    ready_sem,
):
    tok = lax.axis_index("tok")
    head = lax.axis_index("head")
    nxt = (lax.rem(tok + 1, tok_count), head)
    prv = (lax.rem(tok + tok_count - 1, tok_count), head)
    has_prev = tok > 0
    has_next = tok < tok_count - 1

    def rank(h):
        return h + jnp.where((tok == 0) & (h == 0), head_count, 0)

    others = [lax.rem(head + j, head_count) for j in range(1, head_count)]
    mine = rank(head)
    above = [rank(h) > mine for h in others]
    earlier_rank = head + jnp.where((tok == 1) & (head == 0), head_count, 0)
    straight = [has_next & (h < mine) for h in others]
    greeted = [has_prev & ((h > head) | ((tok == 1) & (h == 0))) for h in others]
    relayed = [has_prev & (h > earlier_rank) for h in others]

    def total(flags):
        return sum(flag.astype(jnp.int32) for flag in flags)

    barrier = pltpu.get_barrier_semaphore()

    def signal(semaphore, device):
        pl.semaphore_signal(semaphore, inc=1, device_id=device, device_id_type=MESH)

    pl.when(has_next)(lambda: signal(barrier, nxt))
    pl.when(has_prev)(lambda: signal(barrier, prv))
    for h, flag, flag_prev in zip(others, above, greeted):
        pl.when(flag_prev)(functools.partial(signal, barrier, (prv[0], h)))
        pl.when(flag)(functools.partial(signal, barrier, (tok, h)))

    loads = [
        pltpu.make_async_copy(src, dst, local_sem.at[i])
        for i, (src, dst) in enumerate(
            [(ids_hbm, id_raw), (k_hbm, k_own), (v_hbm, v_own), (q_hbm, qf), (g_hbm, gf)]
        )
    ]
    for load in loads:
        load.start()

    @pl.when(jnp.logical_not(has_prev))
    def _():
        k_prev[...] = jnp.zeros_like(k_prev)
        v_prev[...] = jnp.zeros_like(v_prev)
        for h in range(head_count):
            id_got[head_count + h] = jnp.full_like(id_mine, -1.0)

    @pl.when(jnp.logical_not(has_next))
    def _():
        gk_in[...] = jnp.zeros_like(gk_in)
        gv_in[...] = jnp.zeros_like(gv_in)

    spread = (
        lax.broadcasted_iota(jnp.int32, (IDS, TILE), 1) % IDS
        == lax.broadcasted_iota(jnp.int32, (IDS, TILE), 0)
    )
    loads[0].wait()
    ids = jnp.broadcast_to(id_raw[...].astype(f32), (8, IDS)).astype(bf16)
    id_mine[...] = dot_nn(ids, jnp.where(spread, 1.0, 0.0).astype(bf16))
    id_got[head] = id_mine[...]

    pl.semaphore_wait(barrier, head_count - 1 - total(above) + total([has_next, has_prev, *straight]))

    def send_ids(device, i, src, slot, sent=None):
        return pltpu.make_async_remote_copy(
            src_ref=src,
            dst_ref=id_got.at[slot],
            send_sem=id_send_sem.at[i if sent is None else sent],
            recv_sem=id_recv_sem.at[i],
            device_id=device,
            device_id_type=MESH,
        )

    slot = head_count + head
    ids_next = send_ids(nxt, 0, id_mine, slot)
    ids_beside = [send_ids((tok, h), 1 + j, id_mine, head) for j, h in enumerate(others)]
    ids_straight = [
        send_ids((nxt[0], h), head_count + j, id_mine, slot, 2 * head_count + j)
        for j, h in enumerate(others)
    ]
    ids_on = [
        send_ids((tok, h), head_count + j, id_got.at[slot], slot) for j, h in enumerate(others)
    ]

    def to(device, i, src, dst):
        return pltpu.make_async_remote_copy(
            src_ref=src,
            dst_ref=dst,
            send_sem=send_sem.at[i],
            recv_sem=recv_sem.at[i],
            device_id=device,
            device_id_type=MESH,
        )

    send_k = to(nxt, 0, k_hbm, k_prev)
    send_v = to(nxt, 1, v_hbm, v_prev)
    halves = [pl.ds(t * TILE, TILE) for t in range(TASKS)]
    send_gv = [to(prv, 2 + t, gv_out.at[r], gv_in.at[r]) for t, r in enumerate(halves)]
    send_gk = [to(prv, 4 + t, gk_out.at[r], gk_in.at[r]) for t, r in enumerate(halves)]

    @pl.when(has_next)
    def _():
        ids_next.start()
        for copy, flag in zip(ids_straight, straight):
            pl.when(flag)(copy.start)
        send_k.start()
        send_v.start()

    for h, copy, flag in zip(others, ids_beside, above):

        @pl.when(jnp.logical_not(flag))
        def _():
            signal(ready_sem, (tok, h))
            copy.start()

    def pack_k(k, base):
        a, b, c = parts3(k)
        kc[base : base + 2 * TILE] = lanes(a, a, b, b, c, a)

    def pack_v(v, base):
        a, b = parts2(v)
        vc[base : base + 2 * TILE] = lanes(a, a, b, b)

    def turn(k, v, base):
        kt[:, base : base + 2 * TILE] = rows(*parts2(k.T))
        vt[:, base : base + 2 * TILE] = rows(*parts2(v.T))

    loads[1].wait()
    loads[2].wait()
    pack_k(k_own[...], 2 * TILE)
    pack_v(v_own[...], 2 * TILE)
    loads[3].wait()
    loads[4].wait()

    waiting = total(above)

    @pl.when(waiting > 0)
    def _():
        pl.semaphore_wait(ready_sem, waiting)

    for copy, flag in zip(ids_beside, above):
        pl.when(flag)(copy.start)

    def q_pack(t, pair):
        a, b, c = (qp[t, pair, :, i * TILE : (i + 1) * TILE] for i in range(3))
        return lanes(a, b, a, b, a, c)

    def g_pack(t, pair):
        g = gp[t, pair]
        return lanes(g, g)

    def own_scores(pair, _):
        columns = pl.ds(pl.multiple_of(pair * 2 * TILE, 2 * TILE), 2 * TILE)
        for t in range(TASKS):
            of_task = slice(t * TILE, (t + 1) * TILE)
            q = qf[of_task, columns] * (SCORE_SCALE * LOG2E)
            qp[t, pair] = lanes(*parts3(rows(q[:, :TILE], q[:, TILE:])))
            g = gf[of_task, columns]
            gp[t, pair] = lanes(*parts2(rows(g[:, :TILE], g[:, TILE:])))
            own = slice(2 * TILE, (3 + t) * TILE)
            kept = slice(t * TILE, (1 + 2 * t) * TILE)
            s_own[pair, kept] = dot_nt(kc[own], q_pack(t, pair))
            dp_own[pair, kept] = dot_nt(vc[own], g_pack(t, pair))
        return 0

    lax.fori_loop(0, PAIRS, own_scores, 0, unroll=True)

    @pl.when(has_prev)
    def _():
        ids_next.wait_recv()
        for copy, flag in zip(ids_on, relayed):
            pl.when(flag)(copy.start)


    lane_group = lax.broadcasted_iota(jnp.int32, (8, TILE), 1) // IDS
    per_tile = TILE // IDS

    def id_row(first):
        row = id_got[first]
        for j in range(1, per_tile):
            row = jnp.where(lane_group == j, id_got[first + j], row)
        return jnp.broadcast_to(row[0:1], (TILE, TILE))

    for copy in ids_beside:
        copy.wait_recv()
    of_queries = [id_row(0), id_row(per_tile)]
    causal = lax.broadcasted_iota(jnp.int32, (TILE, TILE), 0) <= lax.broadcasted_iota(
        jnp.int32, (TILE, TILE), 1
    )

    def set_bias(t, j, allowed):
        bias[t, j * TILE : (j + 1) * TILE] = jnp.where(allowed, 0.0, NEG)

    for t in range(TASKS):
        set_bias(t, 2, (of_queries[t].T == of_queries[t]) & causal)
    set_bias(1, 1, of_queries[0].T == of_queries[1])

    def own_weights(pair, _):
        for t in range(TASKS):
            kept = slice(t * TILE, (1 + 2 * t) * TILE)
            b = bias[t, (2 - t) * TILE :]
            s = s_own[pair, kept] + lanes(b, b)
            top = jnp.max(s, axis=0, keepdims=True)
            w = jnp.exp2(s - top)
            s_own[pair, kept] = w
            own_top[t, pair] = top
            own_sum[t, pair] = jnp.sum(w, axis=0, keepdims=True)
            own_dot[t, pair] = jnp.sum(w * dp_own[pair, kept], axis=0, keepdims=True)
        return 0

    lax.fori_loop(0, PAIRS, own_weights, 0, unroll=True)

    pl.when(has_prev)(send_k.wait_recv)
    pack_k(k_prev[...], 0)

    acc_k[...] = jnp.zeros_like(acc_k)
    acc_v[...] = jnp.zeros_like(acc_v)

    def earlier_scores(pair, _):
        for t in range(TASKS):
            before = slice(t * TILE, 2 * TILE)
            pf[t, pair, : (2 - t) * TILE] = dot_nt(kc[before], q_pack(t, pair))
        return 0

    lax.fori_loop(0, PAIRS, earlier_scores, 0, unroll=True)

    @pl.when(has_prev)
    def _():
        for copy in ids_on:
            copy.wait_recv()

    of_keys = [id_row(head_count).T, id_row(head_count + per_tile).T]
    set_bias(0, 0, of_keys[0] == of_queries[0])
    set_bias(0, 1, of_keys[1] == of_queries[0])
    set_bias(1, 0, of_keys[1] == of_queries[1])

    def probs(t, pair, _):
        before = slice(t * TILE, 2 * TILE)
        kept = slice(t * TILE, (1 + 2 * t) * TILE)
        ahead = (2 - t) * TILE
        b = bias[t, :ahead]
        s_prev = pf[t, pair, :ahead] + lanes(b, b)
        top = jnp.maximum(own_top[t, pair], jnp.max(s_prev, axis=0, keepdims=True))
        w_prev = jnp.exp2(s_prev - top)
        shrink = jnp.exp2(own_top[t, pair] - top)
        inv = 1.0 / (jnp.sum(w_prev, axis=0, keepdims=True) + own_sum[t, pair] * shrink)
        inverse[t, pair] = inv * shrink
        p = w_prev * inv
        pf[t, pair, :ahead] = p
        high, low = parts2(p)
        p1[t, pair, :ahead] = high
        p2[t, pair, :ahead] = low
        g = gp[t, pair]
        acc_v[before] += dot_nn(lanes(high, low), rows(g, g))
        return 0

    for t in range(TASKS):
        lax.fori_loop(0, PAIRS, functools.partial(probs, t), 0, unroll=True)
        tile = slice(t * TILE, (t + 1) * TILE)
        gv_out[tile] = acc_v[tile, :TILE] + acc_v[tile, TILE:]
        pl.when(has_prev)(send_gv[t].start)

    pl.when(has_prev)(send_v.wait_recv)
    pack_v(v_prev[...], 0)

    def grads(t, pair, _):
        before = slice(t * TILE, 2 * TILE)
        kept = slice(t * TILE, (1 + 2 * t) * TILE)
        ahead = (2 - t) * TILE
        dp = dot_nt(vc[before], g_pack(t, pair))
        p = pf[t, pair, :ahead]
        row_delta = own_dot[t, pair] * inverse[t, pair] + jnp.sum(p * dp, axis=0, keepdims=True)
        delta[t, pair] = row_delta
        high, low = parts2(p * (dp - row_delta))
        ds1[t, pair, :ahead] = high
        ds2[t, pair, :ahead] = low
        q = qp[t, pair, :, : 2 * TILE]
        acc_k[before] += dot_nn(lanes(high, low), rows(q, q))
        return 0

    for t in range(TASKS):
        lax.fori_loop(0, PAIRS, functools.partial(grads, t), 0, unroll=True)
        tile = slice(t * TILE, (t + 1) * TILE)
        gk_out[tile] = (acc_k[tile, :TILE] + acc_k[tile, TILE:]) * (1.0 / LOG2E)
        pl.when(has_prev)(send_gk[t].start)

    turn(k_prev[...], v_prev[...], 0)
    turn(k_own[...], v_own[...], 2 * TILE)

    def results(pair, _):
        for t in range(TASKS):
            own = slice(2 * TILE, (3 + t) * TILE)
            kept = slice(t * TILE, (1 + 2 * t) * TILE)
            ahead = (2 - t) * TILE
            p = s_own[pair, kept] * inverse[t, pair]
            p_high, p_low = parts2(p)
            d_high, d_low = parts2(p * (dp_own[pair, kept] - delta[t, pair]))
            g = gp[t, pair]
            acc_v[own] += dot_nn(lanes(p_high, p_low), rows(g, g))
            q = qp[t, pair, :, : 2 * TILE]
            acc_k[own] += dot_nn(lanes(d_high, d_low), rows(q, q))
            window = slice(t * TILE, (t + 3) * TILE)
            of_task = slice(t * TILE, (t + 1) * TILE)
            for mat, first, second, high, low, out, scale in (
                (vt, p1, p2, p_high, p_low, o_ref, None),
                (kt, ds1, ds2, d_high, d_low, dq_ref, SCORE_SCALE),
            ):
                m = mat[:, window]
                both = dot_nn(
                    lanes(m, m),
                    rows(first[t, pair, :ahead], high, second[t, pair, :ahead], low),
                )
                x = both[:TILE] + both[TILE:]
                if scale is not None:
                    x = x * scale
                for h in range(2):
                    columns = pl.ds(
                        pl.multiple_of(pair * 2 * TILE + h * TILE, TILE), TILE
                    )
                    out[of_task, columns] = x[:, h * TILE : (h + 1) * TILE].T
        return 0

    lax.fori_loop(0, PAIRS, results, 0, unroll=True)

    dv_own = acc_v[2 * TILE :, :TILE] + acc_v[2 * TILE :, TILE:]
    dk_own = (acc_k[2 * TILE :, :TILE] + acc_k[2 * TILE :, TILE:]) * (1.0 / LOG2E)
    for own, sent, got, out in ((dv_own, send_gv, gv_in, dv_ref), (dk_own, send_gk, gk_in, dk_ref)):
        for t in range(TASKS):
            tile = slice(t * TILE, (t + 1) * TILE)
            pl.when(has_next)(sent[t].wait_recv)
            out[tile] = own[tile] + got[tile]
    for copy in ids_beside:
        copy.wait_send()
    for copy in (ids_next, send_k, send_v):
        pl.when(has_next)(copy.wait_send)
    for copy in (*send_gk, *send_gv):
        pl.when(has_prev)(copy.wait_send)
    for copy, flag in zip((*ids_on, *ids_straight), (*relayed, *straight)):
        pl.when(flag)(copy.wait_send)


def place(a, b, c, d, a_out, b_out, c_out, d_out, sem):
    copies = [
        pltpu.make_async_copy(src, dst, sem.at[i])
        for i, (src, dst) in enumerate([(a, a_out), (b, b_out), (c, c_out), (d, d_out)])
    ]
    for copy in copies:
        copy.start()
    for copy in copies:
        copy.wait()


def per_device(queries, keys, values, cotangent, doc_ids):
    tok_count = lax.axis_size("tok")
    head_count = lax.axis_size("head")
    vmem = pl.BlockSpec(memory_space=pltpu.VMEM)
    hbm = pl.BlockSpec(memory_space=pl.ANY)
    own = 2 * TILE
    win = 3 * TILE
    V = pltpu.VMEM
    found = pl.pallas_call(
        functools.partial(kernel, tok_count, head_count),
        out_shape=(
            jax.ShapeDtypeStruct(queries.shape, f32),
            jax.ShapeDtypeStruct(queries.shape, f32),
            jax.ShapeDtypeStruct(keys.shape, f32),
            jax.ShapeDtypeStruct(keys.shape, f32),
        ),
        in_specs=[hbm] * 5,
        out_specs=(vmem, vmem, vmem, vmem),
        scratch_shapes=[
            V(queries.shape, f32),
            V(queries.shape, f32),
            *[V(keys.shape, f32) for _ in range(8)],
            V((1, IDS), jnp.int32),
            V((8, TILE), f32),
            V((2 * head_count, 8, TILE), f32),
            V((TASKS, win, TILE), f32),
            V((TASKS, PAIRS, own, 3 * TILE), bf16),
            V((TASKS, PAIRS, own, 2 * TILE), bf16),
            V((2 * own, 6 * TILE), bf16),
            V((2 * own, 4 * TILE), bf16),
            V((2 * TILE, 2 * own), bf16),
            V((2 * TILE, 2 * own), bf16),
            V((PAIRS, win, own), f32),
            V((PAIRS, win, own), f32),
            *[V((TASKS, PAIRS, 1, own), f32) for _ in range(5)],
            V((TASKS, PAIRS, own, own), f32),
            *[V((TASKS, PAIRS, own, own), bf16) for _ in range(4)],
            V((2 * own, 2 * TILE), f32),
            V((2 * own, 2 * TILE), f32),
            pltpu.SemaphoreType.DMA((5,)),
            pltpu.SemaphoreType.DMA((6,)),
            pltpu.SemaphoreType.DMA((6,)),
            pltpu.SemaphoreType.DMA((3 * head_count,)),
            pltpu.SemaphoreType.DMA((2 * head_count,)),
            pltpu.SemaphoreType.REGULAR,
        ],
        compiler_params=pltpu.CompilerParams(
            collective_id=0, has_side_effects=True, vmem_limit_bytes=40 * 1024 * 1024
        ),
    )(
        *(
            pltpu.with_memory_space_constraint(x, pltpu.HBM)
            for x in (queries, keys, values, cotangent, doc_ids.reshape(1, IDS))
        )
    )
    return pl.pallas_call(
        place,
        out_shape=tuple(jax.ShapeDtypeStruct(x.shape, f32) for x in found),
        in_specs=[hbm] * 4,
        out_specs=(hbm,) * 4,
        scratch_shapes=[pltpu.SemaphoreType.DMA((4,))],
        compiler_params=pltpu.CompilerParams(vmem_limit_bytes=1024 * 1024),
    )(*found)


def solution(mesh):
    placed = (
        P("tok", "head"),
        P("tok", "head"),
        P("tok", "head"),
        P("tok", "head"),
        P(("tok", "head")),
    )
    return jax.shard_map(
        per_device,
        mesh=mesh,
        in_specs=placed,
        out_specs=(P("tok", "head"), P("tok", "head"), P("tok", "head"), P("tok", "head")),
        check_vma=False,
    )
```
